512 devices in a mesh: section: 4 (over x), tensor: 8 (over y, core), dp: 16 (over z).
Axes of the slice: x: 4, y: 4, z: 16, core: 2. Of those that a mesh axis runs over, the one named last changes fastest.
Arguments:
- inputs: bfloat16 [4, 640, 3072], P(None, 'dp', 'tensor'), may hold values from -6 to 6
- velocity_ref: bfloat16 [4, 640, 3072], P(None, 'dp', 'tensor'), may hold values from -6 to 6
- proj_weights: bfloat16 [4, 3072, 3072], P('section', 'dp', 'tensor'), may hold values from -0.109375 to 0.109375
- section_norm_gains: float32 [4, 3072], P('section'), may hold values from 0.5 to 1.5
- gate_values: float32 [4, 3072], P('section', 'tensor'), may hold values from -4 to 4
- clip_lengths: int32 [16, 4], P('dp'), may hold values from 1 to 40, 100 in all within a row
- step_indices: int32 [16, 4], P('dp'), may hold values from 0 to 49
Outputs:
- grad_weight: float32 [4, 3072, 3072], P('section', 'dp', 'tensor')
- grad_gain: float32 [4, 3072], P('section', 'tensor')
- grad_gate: float32 [4, 3072], P('section', 'tensor')
The draws below stay inside these ranges and needn't reach their ends.
Inputs may be any that keep to these rules, and one draw needn't show every extreme that they name: `clip_lengths`: each clip's lengths over the 4 micro-batches add up to 100, and its longest is exactly 40.
All inputs are finite; a program needn't handle non-finite values.
Results may differ from the reference program's by a relative error of at most 0.02.
Values may be sent and summed in bfloat16 or wider, within the bound.
A program may use at most 128 MiB of HBM per device.

```python
import math
import jax
import jax.numpy as jnp
import numpy as np
from jax import lax

D = 3072
MICRO = 4
CAP = 40
NSTEPS = 50
SECTIONS = 4
CLIPS = 16
COL_BLOCKS = 8
COLS = 384
TOK = 640
LIVE = 1600


def place_ends(values, own_key, smallest, high):
    extent = values.shape
    spot = [jax.random.randint(jax.random.fold_in(own_key, axis), (), 0, extent[axis]) for axis in range(len(extent))]
    values = values.at[tuple(spot)].set(smallest)
    longest = extent.index(max(extent))
    spot[longest] = (spot[longest] + 1) % extent[longest]
    return values.at[tuple(spot)].set(high)


def spiked(entries, rng, source, target, parts, factor):
    def block_of(dim):
        return (jnp.arange(entries.shape[dim]) // (entries.shape[dim] // parts)).reshape((-1,) + (1,) * (entries.ndim - 1 - dim))

    first = jax.random.permutation(rng, parts)[block_of(target)]
    far = (block_of(target) + parts // 2) % parts
    return jnp.where((block_of(source) == first) | (block_of(source) == far), factor * entries, entries)


def block_scale(own_key, dims, cuts, least, high):
    def one(position, shards_of):
        steps = jax.random.uniform(jax.random.fold_in(jax.random.fold_in(own_key, 6), position), (shards_of,), jnp.float32, least / len(cuts), high / len(cuts))
        return jnp.repeat(jnp.exp(steps), dims[position] // shards_of).reshape((-1,) + (1,) * (len(dims) - position - 1))

    factor_of = one(*cuts[0])
    for cut in cuts[1:]:
        factor_of = factor_of * one(*cut)
    return factor_of


def split_up(number_of, total, most, slope):
    loads = [(1 << 20) // math.isqrt(rank ** slope) + 1 for rank in range(2, number_of + 1)]
    surplus, given = total - most - (number_of - 1), [1] * (number_of - 1)
    while surplus > 0:
        free = [i for i in range(number_of - 1) if given[i] < most]
        whole, budget = sum([loads[i] for i in free]), surplus
        for i in free:
            addition = min(most - given[i], max(1, budget * loads[i] // whole), surplus)
            given[i] = given[i] + addition
            surplus = surplus - addition
    return np.array([most] + given)


def ragged_sizes(own_key, amount, total, limit, skew):
    if amount == 2:
        one = jax.random.randint(own_key, (), max(1, total - limit), min(limit, total - 1) + 1)
        return jnp.stack([one, total - one])
    sizes = jnp.asarray(split_up(amount, total, limit, skew), jnp.int32)
    couples = (amount - 1) // 2
    giver, receiver = sizes[1:1 + 2 * couples:2], sizes[2:2 + 2 * couples:2]
    margin = jnp.minimum(giver - 1, limit - receiver)
    shifted = jax.random.randint(jax.random.fold_in(own_key, 1), (couples,), 0, 1 << 20) % (margin + 1)
    sizes = sizes.at[1:1 + 2 * couples:2].set(giver - shifted).at[2:2 + 2 * couples:2].set(receiver + shifted)
    return sizes[jax.random.permutation(jax.random.fold_in(own_key, 2), amount)]


def normal_values(key, shape, spread, most, pieces=(), held_as=jnp.bfloat16):
    entries = jax.random.normal(key, shape, jnp.float32) * spread
    if len(pieces) > 0:
        entries = block_scale(key, shape, pieces, -0.22, 0.18) * entries
    return jnp.clip(entries, min=-most, max=most).astype(held_as)


def bell_draw_with(key, shape, scale, reach, split, heavy, kind=jnp.bfloat16):
    entries = scale * jax.random.normal(key, shape, jnp.float32)
    if split:
        entries = entries * block_scale(key, shape, split, -0.22, 0.18)
    return jnp.clip(spiked(entries, jax.random.fold_in(key, 3), *heavy), -reach, reach).astype(kind)


def setup_inputs(seed: int = 0) -> dict:
    keys = jax.random.split(jax.random.key(seed), 8)
    return {
        "inputs": bell_draw_with(keys[0], (MICRO, TOK, D), 1.0, 6.0, ((1, 16), (2, 8)), (1, 2, 16, 2.0)),
        "velocity_ref": normal_values(keys[1], (MICRO, TOK, D), 1.0, 6.0, ((1, 16), (2, 8))),
        "proj_weights": normal_values(keys[2], (SECTIONS, D, D), D ** -0.5, 0.109375, ((0, 4), (1, 16), (2, 8))),
        "section_norm_gains": jnp.clip(1.0 + 0.1 * jax.random.normal(keys[3], (SECTIONS, D), jnp.float32), 0.5, 1.5),
        "gate_values": normal_values(keys[4], (SECTIONS, D), 1.0, 4.0, ((0, 4), (1, 8)), jnp.float32),
        "clip_lengths": jax.vmap(lambda own: ragged_sizes(own, MICRO, 5 * CAP // 2, CAP, 2))(jax.random.split(keys[5], CLIPS)).reshape((CLIPS, MICRO)).astype(jnp.int32),
        "step_indices": place_ends(jax.random.randint(keys[6], (CLIPS, MICRO), 0, NSTEPS), jax.random.fold_in(keys[6], 1), 0, NSTEPS - 1).astype(jnp.int32),
    }


EPS = 1e-06

def gelu_slope(values):
    coeff = math.sqrt(2.0 / math.pi)
    tanh_val = jnp.tanh(coeff * (values + 0.044715 * values * values * values))
    return 0.5 * (1.0 + tanh_val) + 0.5 * values * (1.0 - tanh_val * tanh_val) * coeff * (1.0 + 3.0 * 0.044715 * values * values)

def apply_normalization(rows_in):
    mean_val = lax.optimization_barrier(jnp.mean(rows_in, axis=-1, keepdims=True))
    mean_removed = rows_in - mean_val
    inverse_deviation = lax.rsqrt(lax.optimization_barrier(jnp.mean(mean_removed * mean_removed, axis=-1, keepdims=True)) + EPS)
    return (mean_removed * inverse_deviation, inverse_deviation)

def add_clip(total, pair):
    left, right = pair
    term = jnp.dot(left.T, right, preferred_element_type=jnp.float32)
    rounded = lax.optimization_barrier(term.astype(jnp.bfloat16))
    return (total + rounded.astype(jnp.float32), None)

def reference(inputs, velocity_ref, proj_weights, section_norm_gains, gate_values, clip_lengths, step_indices):
    positions = jnp.arange(CAP, dtype=jnp.int32)
    live_mask = (positions[None, None, :] < clip_lengths.T[:, :, None]).astype(jnp.float32)
    weighting = 1.0 / (0.1 + (step_indices.T.astype(jnp.float32) + 0.5) / NSTEPS)
    factor = (live_mask * weighting[:, :, None]).reshape(MICRO, TOK) / math.sqrt(LIVE)
    carry_state = inputs
    stored_values = []
    for section_index in range(SECTIONS):
        standardized, inverse_deviation = apply_normalization(carry_state.astype(jnp.float32))
        normed_rows = (standardized * section_norm_gains[section_index]).astype(jnp.bfloat16)
        projection_output = jnp.dot(normed_rows.reshape(MICRO * TOK, D), proj_weights[section_index], preferred_element_type=jnp.float32).reshape(MICRO, TOK, D)
        carry_state = (carry_state.astype(jnp.float32) + gate_values[section_index] * jax.nn.gelu(projection_output, approximate=True)).astype(jnp.bfloat16)
        stored_values.append((standardized, inverse_deviation, normed_rows, projection_output))
    upstream_gradient = (factor[:, :, None] * (carry_state.astype(jnp.float32) - velocity_ref.astype(jnp.float32))).astype(jnp.bfloat16)
    weight_list = []
    gain_entries = []
    gate_list = []
    for section_index in reversed(range(SECTIONS)):
        standardized, inverse_deviation, normed_rows, projection_output = stored_values[section_index]
        arriving_input = upstream_gradient.astype(jnp.float32)
        gate_list.append(lax.optimization_barrier(jnp.sum(arriving_input * jax.nn.gelu(projection_output, approximate=True), axis=(0, 1))))
        dproj = (arriving_input * gate_values[section_index] * gelu_slope(projection_output)).astype(jnp.bfloat16)
        normed_clips = normed_rows.reshape(MICRO, CLIPS, CAP, D).transpose(1, 0, 2, 3).reshape(CLIPS, MICRO * CAP, D)
        dproj_clips = dproj.reshape(MICRO, CLIPS, CAP, D).transpose(1, 0, 2, 3).reshape(CLIPS, MICRO * CAP, D)
        weight_grad, _ = lax.scan(add_clip, jnp.zeros((D, D), jnp.float32), (normed_clips, dproj_clips))
        weight_list.append(weight_grad)
        flat_rows = dproj.reshape(MICRO * TOK, COL_BLOCKS, COLS).astype(jnp.float32)
        weight_blocks = proj_weights[section_index].reshape(D, COL_BLOCKS, COLS).astype(jnp.float32)
        partial_value = jnp.einsum('rtk,dtk->trd', flat_rows, weight_blocks)
        rounded = lax.optimization_barrier(partial_value.astype(jnp.bfloat16))
        normed_gradient = lax.optimization_barrier(jnp.sum(rounded.astype(jnp.float32), axis=0)).reshape(MICRO, TOK, D)
        gain_entries.append(lax.optimization_barrier(jnp.sum(normed_gradient * standardized, axis=(0, 1))))
        scaled_rows = normed_gradient * section_norm_gains[section_index]
        first_moment = lax.optimization_barrier(jnp.mean(scaled_rows, axis=-1, keepdims=True))
        second_moment = lax.optimization_barrier(jnp.mean(scaled_rows * standardized, axis=-1, keepdims=True))
        upstream_gradient = (arriving_input + inverse_deviation * (scaled_rows - first_moment - standardized * second_moment)).astype(jnp.bfloat16)
    return (jnp.stack(weight_list[::-1]), jnp.stack(gain_entries[::-1]), jnp.stack(gate_list[::-1]))
```

```python
import functools
import math

import jax
import jax.numpy as jnp
from jax import lax
from jax.experimental import pallas as pl
from jax.experimental.pallas import tpu as pltpu
from jax.sharding import PartitionSpec as P

MESH = pl.DeviceIdType.MESH
F32 = jnp.float32
BF16 = jnp.bfloat16
NSTEPS = 50
LIVE_PER_CLIP = 100
EPS = 1e-06
LANES = 128
HALVES = 2
SMALL_ROWS = 24
TAIL = 16
PARTS_AT = 124
LAG = 3


def split3(value):
    first = value.astype(BF16)
    rest = value - first.astype(F32)
    second = rest.astype(BF16)
    third = (rest - second.astype(F32)).astype(BF16)
    return first, second, third


def stat_rows(one, two):
    rows = [r.astype(F32) for r in split3(one) + split3(two)]
    rows.append(jnp.zeros((TAIL - 6, LANES), F32))
    return jnp.concatenate(rows, axis=0).astype(BF16)


def joined(block):
    block = block.astype(F32)
    one = block[0:1] + block[1:2] + block[2:3]
    two = block[3:4] + block[4:5] + block[5:6]
    return one, two


def kernel(
    nx, nt, nz,
    w_in, inputs, velocity, gains, gates, lengths, steps,
    gw_out, gain_out, gate_out,
    wbuf, wt, small_src, small, gainb, gtail, gateb, picked, abuf, bsend, bbuf,
    projb, gelub, slopeb, meanb, invb, ub, dbuf, qsend, qbuf, dwbuf, rs_up, rs_down,
    gw_send, gw_in, vacc, v1, v2, v3,
    send_sem, local_sem, w_sem, small_sem, up_sem, down_sem, a_sem, b_sem, d_sem, q_sem,
    rsu_sem, rsd_sem, gw_sem, v1_sem, v2_sem, v3_sem,
):
    sections = nx
    chunk = gates.shape[1] // (HALVES * nx)
    width = gates.shape[1]
    own = HALVES * chunk
    deep = nt * own
    model = nt * width
    ups, downs = nz // 2, nz // 2 - 1
    zb = 4
    za = nz // zb
    x = lax.axis_index("section")
    t = lax.axis_index("tensor")
    z = lax.axis_index("dp")
    above = lax.rem(z + 1, nz)
    below = lax.rem(z + nz - 1, nz)
    group, member = z // zb, lax.rem(z, zb)

    small[...] = jnp.zeros_like(small)
    barrier = pltpu.get_barrier_semaphore()
    greeted = 0

    def greet(axis, index):
        pl.semaphore_signal(barrier, inc=1, device_id={axis: index}, device_id_type=MESH)

    for d in range(1, nx):
        greet("section", lax.rem(x + d, nx))
        greeted += 1
    greet("dp", above)
    greet("dp", below)
    greeted += 2
    for d in range(1, nt):
        greet("tensor", lax.rem(t + d, nt))
        greeted += 1
    for d in range(1, zb):
        greet("dp", group * zb + lax.rem(member + d, zb))
        greeted += 1
    for d in range(1, za):
        greet("dp", lax.rem(group + d, za) * zb + member)
        greeted += 1

    sends = []

    def put(src, dst, recv, axis, index):
        copy = pltpu.make_async_remote_copy(
            src_ref=src, dst_ref=dst, send_sem=send_sem.at[len(sends)], recv_sem=recv,
            device_id={axis: index}, device_id_type=MESH,
        )
        copy.start()
        sends.append(copy)

    def got(dst, recv):
        pltpu.make_async_remote_copy(
            src_ref=dst, dst_ref=dst, send_sem=send_sem.at[0], recv_sem=recv,
            device_id={"dp": above}, device_id_type=MESH,
        ).wait_recv()

    own_rows = pl.ds(pl.multiple_of(x * chunk, 16), chunk)
    keep = pltpu.make_async_copy(w_in.at[0, own_rows], wbuf.at[x, z], local_sem.at[0])
    keep.start()
    small_src[...] = jnp.zeros_like(small_src)
    for to in range(nx):
        for unit in range(nz):
            at = unit * (width // HALVES) + to * chunk
            small_src[to, unit:unit + 1, 0:chunk] = gains[0:1, at:at + chunk]
        for half in range(HALVES):
            at = half * (width // HALVES) + to * chunk
            small_src[to, 16 + half:17 + half, 0:chunk] = gates[0:1, at:at + chunk]

    pl.semaphore_wait(barrier, greeted)

    for d in range(1, nx):
        to = lax.rem(x + d, nx)
        rows = pl.ds(pl.multiple_of(to * chunk, 16), chunk)
        put(w_in.at[0, rows], wbuf.at[x, z], w_sem.at[x], "section", to)
    small_at = pl.ds(pl.multiple_of(x * SMALL_ROWS, 8), SMALL_ROWS)
    for d in range(1, nx):
        to = lax.rem(x + d, nx)
        put(small_src.at[to], small.at[small_at], small_sem.at[x], "section", to)
    small[small_at] = small_src[x]
    keep.wait()

    def wait_piece(s):
        @pl.when(x != s)
        def _():
            got(wbuf.at[s, z], w_sem.at[s])

    def gather_send(s, k):
        if k <= ups:
            piece = wbuf.at[s, lax.rem(z - k + 1 + nz, nz)]
            put(piece, piece, up_sem.at[s, k - 1], "dp", above)
        if k <= downs:
            piece = wbuf.at[s, lax.rem(z + k - 1, nz)]
            put(piece, piece, down_sem.at[s, k - 1], "dp", below)

    def gather_event(s, k):
        if k == 0:
            wait_piece(s)
        else:
            if k <= ups:
                got(wbuf.at[s, lax.rem(z - k + nz, nz)], up_sem.at[s, k - 1])
            if k <= downs:
                got(wbuf.at[s, lax.rem(z + k, nz)], down_sem.at[s, k - 1])
        gather_send(s, k + 1)

    events = sorted((k + LAG * s, s, k) for s in range(sections) for k in range(ups + 1))

    def gather_until(key):
        while events and events[0][0] <= key:
            _, s, k = events.pop(0)
            gather_event(s, k)

    gather_until(0)

    lane = lax.broadcasted_iota(jnp.int32, (own, LANES), 1)

    micro, cap = inputs.shape[0], inputs.shape[1]
    slot = lax.broadcasted_iota(jnp.int32, (cap, LANES), 1)
    row = lax.broadcasted_iota(jnp.int32, (cap, LANES), 0)
    first = jnp.int32(0)
    factor = jnp.zeros((own, LANES), F32)
    start_block = jnp.zeros((width, LANES), F32)
    target_block = jnp.zeros((width, LANES), F32)
    over_rows = (((0,), (0,)), ((), ()))
    for m in range(micro):
        count = lengths[0, m]
        chosen = jnp.where((slot - row == first) & (row < count), 1.0, 0.0).astype(BF16)
        start_block += lax.dot_general(inputs[m], chosen, over_rows, preferred_element_type=F32)
        target_block += lax.dot_general(velocity[m], chosen, over_rows, preferred_element_type=F32)
        step = jnp.broadcast_to(steps[0, m], (own, LANES)).astype(F32)
        weighting = 1.0 / (0.1 + (step + 0.5) / NSTEPS)
        inside = (lane >= first) & (lane < first + count)
        factor = jnp.where(inside, weighting / math.sqrt(LIVE_PER_CLIP * nz), factor)
        first = first + count
    picked[0] = start_block.astype(BF16).reshape(HALVES * nx, chunk, LANES)
    picked[1] = target_block.astype(BF16).reshape(HALVES * nx, chunk, LANES)

    def own_part(which):
        return jnp.concatenate([picked[which, half * nx + x] for half in range(HALVES)], axis=0)

    abuf[0, t] = own_part(0)

    def a_sends(s):
        for d in range(1, nt):
            put(abuf.at[s, t], abuf.at[s, t], a_sem.at[s, t], "tensor", lax.rem(t + d, nt))

    a_sends(0)
    gather_until(1)

    for d in range(1, nx):
        at = lax.rem(x + d, nx)
        got(small.at[pl.ds(pl.multiple_of(at * SMALL_ROWS, 8), SMALL_ROWS)], small_sem.at[at])
    columns = jnp.transpose(small[...])
    wide_lane = lax.broadcasted_iota(jnp.int32, (chunk, LANES), 1)

    def spread_gains(s):
        for unit in range(nz):
            at = s * SMALL_ROWS + unit
            part = jnp.broadcast_to(columns[0:chunk, at:at + 1], (chunk, LANES))
            gainb[s, unit * chunk:(unit + 1) * chunk] = part
            a, b, c = (p.astype(F32) for p in split3(part))
            tail = jnp.where(wide_lane == PARTS_AT + 1, a, 0.0)
            tail = jnp.where(wide_lane == PARTS_AT + 2, b, tail)
            tail = jnp.where(wide_lane == PARTS_AT + 3, c, tail)
            gtail[s, unit * chunk:(unit + 1) * chunk] = tail
        for half in range(HALVES):
            at = s * SMALL_ROWS + 16 + half
            part = jnp.broadcast_to(columns[0:chunk, at:at + 1], (chunk, LANES))
            gateb[s, half * chunk:(half + 1) * chunk] = part

    for s in range(sections):
        spread_gains(s)
        gather_until(2 + s)

    factor = jnp.where(lane < LIVE_PER_CLIP, factor, 0.0)

    coeff = math.sqrt(2.0 / math.pi)
    state = None
    for s in range(sections):
        if s > 0:
            abuf[s, t] = state
            a_sends(s)
        gather_until(ups + LAG * s)
        weight = wbuf[s].reshape(deep, width)
        wt[...] = jnp.transpose(weight)
        for d in range(1, nt):
            at = lax.rem(t + d, nt)
            got(abuf.at[s, at], a_sem.at[s, at])
        values = abuf[s].reshape(deep, LANES).astype(F32)
        slice_mean = jnp.sum(values, axis=0, keepdims=True) * (1.0 / deep)
        centred = values - slice_mean
        slice_square = jnp.sum(centred * centred, axis=0, keepdims=True)
        operand = (centred * gainb[s] + gtail[s]).astype(BF16)
        partial = jnp.dot(wt[...], operand, preferred_element_type=F32)
        rounding = partial - partial.astype(BF16).astype(F32)
        all_lane = lax.broadcasted_iota(jnp.int32, (width, LANES), 1)
        partial = jnp.where(
            all_lane == PARTS_AT, pltpu.roll(rounding, LANES - 1, 1), partial
        ).astype(BF16)
        stats = stat_rows(slice_mean, slice_square)
        for to in range(nx):
            for half in range(HALVES):
                at = half * (width // HALVES) + to * chunk
                bsend[s, to, half * chunk:(half + 1) * chunk] = partial[at:at + chunk]
            bsend[s, to, own:own + TAIL] = stats
        for d in range(1, nx):
            to = lax.rem(x + d, nx)
            put(bsend.at[s, to], bbuf.at[s, x], b_sem.at[s, x], "section", to)
        bbuf[s, x] = bsend[s, x]
        gather_until(ups + LAG * s + LAG - 1)
        for d in range(1, nx):
            at = lax.rem(x + d, nx)
            got(bbuf.at[s, at], b_sem.at[s, at])
        summed = jnp.zeros((own, LANES), F32)
        means, squares, sums = [], [], []
        for at in range(nx):
            block = bbuf[s, at, 0:own].astype(F32)
            summed += block
            sums.append(
                jnp.sum(jnp.where(lane >= PARTS_AT, block, 0.0), axis=1, keepdims=True)
            )
            one, two = joined(bbuf[s, at, own:own + TAIL])
            means.append(one)
            squares.append(two)
        mean = sum(means[1:], means[0]) * (1.0 / nx)
        square = sum(squares[1:], squares[0])
        for at in range(nx):
            square += deep * (means[at] - mean) * (means[at] - mean)
        inverse = lax.rsqrt(square * (1.0 / model) + EPS)
        total = jnp.where(lane < PARTS_AT, summed, 0.0)
        for at in range(nx):
            total += (means[at] - mean) * sums[at]
        v = total * inverse
        tanh = jnp.tanh(coeff * (v + 0.044715 * v * v * v))
        gelu = 0.5 * v * (1.0 + tanh)
        slope = 0.5 * (1.0 + tanh) + 0.5 * v * (1.0 - tanh * tanh) * coeff * (
            1.0 + 3.0 * 0.044715 * v * v
        )
        gate = gateb[s]
        projb[s] = v
        gelub[s] = gelu
        slopeb[s] = gate * slope
        meanb[s] = mean
        invb[s] = inverse
        ub[s] = jnp.broadcast_to(sum(sums[1:], sums[0]), (own, LANES))
        state = (abuf[s, t].astype(F32) + gate * gelu).astype(BF16)

    gather_until(ups + LAG * sections)

    target = own_part(1).astype(F32)
    upstream = (factor * (state.astype(F32) - target)).astype(BF16).astype(F32)
    vacc[...] = jnp.zeros_like(vacc)

    def scatter_send(s, k):
        if k <= ups:
            src = dwbuf.at[s, lax.rem(z + ups, nz)] if k == 1 else rs_up.at[s, k - 2]
            put(src, rs_up.at[s, k - 1], rsu_sem.at[s, k - 1], "dp", above)
        if k <= downs:
            src = dwbuf.at[s, lax.rem(z + nz - downs, nz)] if k == 1 else rs_down.at[s, k - 2]
            put(src, rs_down.at[s, k - 1], rsd_sem.at[s, k - 1], "dp", below)

    def scatter_event(s, k):
        if k == 0:
            scatter_send(s, 1)
            return
        if k <= ups:
            got(rs_up.at[s, k - 1], rsu_sem.at[s, k - 1])
        if k <= downs:
            got(rs_down.at[s, k - 1], rsd_sem.at[s, k - 1])
        if k < ups:
            mine = dwbuf[s, lax.rem(z + ups - k, nz)].astype(F32)
            rs_up[s, k - 1] = (rs_up[s, k - 1].astype(F32) + mine).astype(BF16)
        if k < downs:
            mine = dwbuf[s, lax.rem(z + nz - downs + k, nz)].astype(F32)
            rs_down[s, k - 1] = (rs_down[s, k - 1].astype(F32) + mine).astype(BF16)
        scatter_send(s, k + 1)
        if k == ups:
            whole = dwbuf[s, z].astype(F32) + rs_up[s, ups - 1].astype(F32)
            if downs > 0:
                whole = whole + rs_down[s, downs - 1].astype(F32)
            gw_send[s] = whole.astype(BF16)

            @pl.when(x != s)
            def _():
                put_to(gw_send.at[s], gw_in.at[x], gw_sem.at[x], s)

            @pl.when(x == s)
            def _():
                gw_in[x] = gw_send[s]

    def put_to(src, dst, recv, s):
        pltpu.make_async_remote_copy(
            src_ref=src, dst_ref=dst, send_sem=local_sem.at[1 + s], recv_sem=recv,
            device_id={"section": s}, device_id_type=MESH,
        ).start()

    back = sorted(
        (k + LAG * (sections - 1 - s), s, k) for s in range(sections) for k in range(ups + 1)
    )

    def scatter_until(key):
        while back and back[0][0] <= key:
            _, s, k = back.pop(0)
            scatter_event(s, k)

    for turn, s in enumerate(reversed(range(sections))):
        vacc[0:own] = jnp.where(
            lane == 2 * s, jnp.sum(upstream * gelub[s], axis=1, keepdims=True), vacc[0:own]
        )
        dproj = (upstream * slopeb[s]).astype(BF16)
        exact = dproj.astype(F32)
        first_part = jnp.sum(exact * ub[s], axis=0, keepdims=True)
        second_part = jnp.sum(exact * projb[s], axis=0, keepdims=True)
        dbuf[s, x, 0:own] = dproj
        dbuf[s, x, own:own + TAIL] = stat_rows(first_part, second_part)
        for d in range(1, nx):
            put(dbuf.at[s, x], dbuf.at[s, x], d_sem.at[s, x], "section", lax.rem(x + d, nx))
        if turn > 0:
            scatter_until(LAG * turn - 2)
        mean, inverse = meanb[s], invb[s]
        normed = (
            (abuf[s].reshape(deep, LANES).astype(F32) - mean) * inverse * gainb[s]
        ).astype(BF16)
        for d in range(1, nx):
            at = lax.rem(x + d, nx)
            got(dbuf.at[s, at], d_sem.at[s, at])
        whole = jnp.concatenate(
            [dbuf[s, at, half * chunk:(half + 1) * chunk] for half in range(HALVES) for at in range(nx)],
            axis=0,
        )
        first_sum = jnp.zeros((1, LANES), F32)
        second_sum = jnp.zeros((1, LANES), F32)
        for at in range(nx):
            one, two = joined(dbuf[s, at, own:own + TAIL])
            first_sum += one
            second_sum += two
        product = jnp.dot(wbuf[s].reshape(deep, width), whole, preferred_element_type=F32).astype(BF16)
        stats = stat_rows(first_sum, second_sum)
        for to in range(nt):
            qsend[s, to, 0:own] = product[to * own:(to + 1) * own]
            qsend[s, to, own:own + TAIL] = stats
        for d in range(1, nt):
            to = lax.rem(t + d, nt)
            put(qsend.at[s, to], qbuf.at[s, t], q_sem.at[s, t], "tensor", to)
        qbuf[s, t] = qsend[s, t]
        term = lax.dot_general(
            normed, whole, (((1,), (1,)), ((), ())), preferred_element_type=F32
        )
        dwbuf[s] = term.astype(BF16).reshape(nz, chunk, width)
        scatter_until(LAG * turn)
        for d in range(1, nt):
            at = lax.rem(t + d, nt)
            got(qbuf.at[s, at], q_sem.at[s, at])
        dnormed = jnp.zeros((own, LANES), F32)
        first_moment = jnp.zeros((1, LANES), F32)
        second_moment = jnp.zeros((1, LANES), F32)
        for at in range(nt):
            dnormed += qbuf[s, at, 0:own].astype(F32)
            one, two = joined(qbuf[s, at, own:own + TAIL])
            first_moment += one
            second_moment += two
        xhat = (abuf[s, t].astype(F32) - mean) * inverse
        vacc[0:own] = jnp.where(
            lane == 2 * s + 1, jnp.sum(dnormed * xhat, axis=1, keepdims=True), vacc[0:own]
        )
        if s > 0:
            gain = gainb[s, pl.ds(pl.multiple_of(t * own, 8), own)]
            change = dnormed * gain - first_moment * (1.0 / model) - xhat * (
                second_moment * (1.0 / model)
            )
            upstream = (upstream + inverse * change).astype(BF16).astype(F32)

    v1[member] = jnp.transpose(vacc[...])[0:8]
    for d in range(1, zb):
        to = group * zb + lax.rem(member + d, zb)
        put(v1.at[member], v1.at[member], v1_sem.at[member], "dp", to)
    scatter_until(LAG * sections - 1)
    for d in range(1, zb):
        at = lax.rem(member + d, zb)
        got(v1.at[at], v1_sem.at[at])
    v2[group] = v1[0] + v1[1] + v1[2] + v1[3]
    for d in range(1, za):
        to = lax.rem(group + d, za) * zb + member
        put(v2.at[group], v2.at[group], v2_sem.at[group], "dp", to)
    scatter_until(LAG * sections)
    for d in range(1, za):
        at = lax.rem(group + d, za)
        got(v2.at[at], v2_sem.at[at])
    full = v2[0]
    for at in range(1, za):
        full = full + v2[at]
    v3[x] = full
    for d in range(1, nx):
        put(v3.at[x], v3.at[x], v3_sem.at[x], "section", lax.rem(x + d, nx))
    scatter_until(LAG * sections + ups)
    for d in range(1, nx):
        at = lax.rem(x + d, nx)
        got(v3.at[at], v3_sem.at[at])
    for at in range(nx):
        tile = v3[at]
        gate_row, gain_row = tile[0:1], tile[1:2]
        for s in range(1, sections):
            gate_row = jnp.where(x == s, tile[2 * s:2 * s + 1], gate_row)
            gain_row = jnp.where(x == s, tile[2 * s + 1:2 * s + 2], gain_row)
        for half in range(HALVES):
            to = half * (width // HALVES) + at * chunk
            gate_out[0:1, to:to + chunk] = gate_row[:, half * chunk:(half + 1) * chunk]
            gain_out[0:1, to:to + chunk] = gain_row[:, half * chunk:(half + 1) * chunk]
    for d in range(1, nx):
        at = lax.rem(x + d, nx)
        got(gw_in.at[at], gw_sem.at[at])
    for at in range(nx):
        gw_out[0, at * chunk:(at + 1) * chunk] = gw_in[at].astype(F32)

    for copy in sends:
        copy.wait_send()
    for s in range(sections):
        @pl.when(x != s)
        def _():
            pltpu.make_async_remote_copy(
                src_ref=gw_send.at[s], dst_ref=gw_in.at[x], send_sem=local_sem.at[1 + s],
                recv_sem=gw_sem.at[x], device_id={"section": s}, device_id_type=MESH,
            ).wait_send()


def local(inputs, velocity, weights, gains, gates, lengths, steps):
    nx, nt, nz = lax.axis_size("section"), lax.axis_size("tensor"), lax.axis_size("dp")
    sections = nx
    width = inputs.shape[2]
    chunk = width // (HALVES * nx)
    own = HALVES * chunk
    deep = nt * own
    ups, downs = nz // 2, nz // 2 - 1
    block = own + TAIL
    sends = (
        2 * (nx - 1) + 2 * sections * (ups + downs) + 2 * sections * (nt - 1)
        + 2 * sections * (nx - 1) + 3 + nz // 4 - 1 + nx - 1
    )
    dma = pltpu.SemaphoreType.DMA
    vmem = pl.BlockSpec(memory_space=pltpu.VMEM)
    smem = pl.BlockSpec(memory_space=pltpu.SMEM)
    return pl.pallas_call(
        functools.partial(kernel, nx, nt, nz),
        out_shape=(
            jax.ShapeDtypeStruct((1, nx * chunk, width), F32),
            jax.ShapeDtypeStruct((1, width), F32),
            jax.ShapeDtypeStruct((1, width), F32),
        ),
        in_specs=[vmem, vmem, vmem, vmem, vmem, smem, smem],
        out_specs=(vmem, vmem, vmem),
        scratch_shapes=[
            pltpu.VMEM((sections, nz, chunk, width), BF16),
            pltpu.VMEM((width, deep), BF16),
            pltpu.VMEM((nx, SMALL_ROWS, LANES), F32),
            pltpu.VMEM((LANES, LANES), F32),
            pltpu.VMEM((sections, deep, LANES), F32),
            pltpu.VMEM((sections, deep, LANES), F32),
            pltpu.VMEM((sections, own, LANES), F32),
            pltpu.VMEM((2, HALVES * nx, chunk, LANES), BF16),
            pltpu.VMEM((sections, nt, own, LANES), BF16),
            pltpu.VMEM((sections, nx, block, LANES), BF16),
            pltpu.VMEM((sections, nx, block, LANES), BF16),
            pltpu.VMEM((sections, own, LANES), F32),
            pltpu.VMEM((sections, own, LANES), F32),
            pltpu.VMEM((sections, own, LANES), F32),
            pltpu.VMEM((sections, 1, LANES), F32),
            pltpu.VMEM((sections, 1, LANES), F32),
            pltpu.VMEM((sections, own, LANES), F32),
            pltpu.VMEM((sections, nx, block, LANES), BF16),
            pltpu.VMEM((sections, nt, block, LANES), BF16),
            pltpu.VMEM((sections, nt, block, LANES), BF16),
            pltpu.VMEM((sections, nz, chunk, width), BF16),
            pltpu.VMEM((sections, ups, chunk, width), BF16),
            pltpu.VMEM((sections, max(downs, 1), chunk, width), BF16),
            pltpu.VMEM((sections, chunk, width), BF16),
            pltpu.VMEM((nx, chunk, width), BF16),
            pltpu.VMEM((LANES, LANES), F32),
            pltpu.VMEM((4, 8, LANES), F32),
            pltpu.VMEM((max(nz // 4, 1), 8, LANES), F32),
            pltpu.VMEM((nx, 8, LANES), F32),
            dma((sends,)),
            dma((1 + sections,)),
            dma((nx,)),
            dma((nx,)),
            dma((sections, ups)),
            dma((sections, max(downs, 1))),
            dma((sections, nt)),
            dma((sections, nx)),
            dma((sections, nx)),
            dma((sections, nt)),
            dma((sections, ups)),
            dma((sections, max(downs, 1))),
            dma((nx,)),
            dma((4,)),
            dma((max(nz // 4, 1),)),
            dma((nx,)),
        ],
        compiler_params=pltpu.CompilerParams(
            collective_id=0, has_side_effects=True, vmem_limit_bytes=48 * 1024 * 1024
        ),
        name="sections",
    )(weights, inputs, velocity, gains, gates, lengths, steps)


def solution(mesh):
    placed = (
        P(None, "dp", "tensor"),
        P(None, "dp", "tensor"),
        P("section", "dp", "tensor"),
        P("section", None),
        P("section", "tensor"),
        P("dp", None),
        P("dp", None),
    )

    def whole(*args):
        return jax.shard_map(
            local, mesh=mesh, in_specs=placed,
            out_specs=(P("section", "dp", "tensor"), P("section", "tensor"), P("section", "tensor")),
            check_vma=False,
        )(*args)

    return whole
```

```python
import functools
import math

import jax
import jax.numpy as jnp
from jax import lax
from jax.experimental import pallas as pl
from jax.experimental.pallas import tpu as pltpu
from jax.sharding import PartitionSpec as P

MESH = pl.DeviceIdType.MESH
F32 = jnp.float32
BF16 = jnp.bfloat16
NSTEPS = 50
LIVE_PER_CLIP = 100
EPS = 1e-06
LANES = 128
HALVES = 2
SMALL_ROWS = 24
TAIL = 16
PARTS_AT = 124
LAG = 2
GATHER_REACH = (2, 2, 2, 2)
SCATTER_REACH = (2, 2, 2, 2)


def split3(value):
    first = value.astype(BF16)
    rest = value - first.astype(F32)
    second = rest.astype(BF16)
    third = (rest - second.astype(F32)).astype(BF16)
    return first, second, third


def stat_rows(one, two):
    rows = [r.astype(F32) for r in split3(one) + split3(two)]
    rows.append(jnp.zeros((TAIL - 6, LANES), F32))
    return jnp.concatenate(rows, axis=0).astype(BF16)


def joined(block):
    block = block.astype(F32)
    one = block[0:1] + block[1:2] + block[2:3]
    two = block[3:4] + block[4:5] + block[5:6]
    return one, two


def kernel(
    nx, nt, nz,
    w_in, inputs_in, velocity_in, gains_in, gates_in, lengths_in, steps_in,
    gw_out, gain_out, gate_out,
    inputs, velocity, gains, gates, lengths, steps,
    wbuf, wt, small_src, small, gainb, gtail, gateb, picked, abuf, bsend, bbuf,
    projb, gelub, slopeb, meanb, invb, ub, dbuf, qsend, qbuf, dwbuf, rs_up, rs_down,
    gw_send, gw_in, vacc, v1, v2, v3,
    send_sem, local_sem, load_sem, w_sem, small_sem, up_sem, down_sem, a_sem, b_sem, d_sem, q_sem,
    rsu_sem, rsd_sem, gw_sem, v1_sem, v2_sem, v3_sem,
):
    sections = nx
    chunk = gates.shape[1] // (HALVES * nx)
    width = gates.shape[1]
    own = HALVES * chunk
    deep = nt * own
    model = nt * width
    ups, downs = nz // 2, nz // 2 - 1
    zb = 4
    za = nz // zb
    x = lax.axis_index("section")
    t = lax.axis_index("tensor")
    z = lax.axis_index("dp")
    above = lax.rem(z + 1, nz)
    group, member = z // zb, lax.rem(z, zb)

    small[...] = jnp.zeros_like(small)
    barrier = pltpu.get_barrier_semaphore()
    greeted = 0

    def greet(axis, index):
        pl.semaphore_signal(barrier, inc=1, device_id={axis: index}, device_id_type=MESH)

    for d in range(1, nx):
        greet("section", lax.rem(x + d, nx))
        greeted += 1
    far = max(GATHER_REACH + SCATTER_REACH)
    for d in range(1, far + 1):
        greet("dp", lax.rem(z + d, nz))
        greet("dp", lax.rem(z + nz - d, nz))
        greeted += 2
    for d in range(1, nt):
        greet("tensor", lax.rem(t + d, nt))
        greeted += 1
    for d in range(1, zb):
        greet("dp", group * zb + lax.rem(member + d, zb))
        greeted += 1
    for d in range(1, za):
        greet("dp", lax.rem(group + d, za) * zb + member)
        greeted += 1

    sends = []

    def put(src, dst, recv, axis, index):
        copy = pltpu.make_async_remote_copy(
            src_ref=src, dst_ref=dst, send_sem=send_sem.at[len(sends)], recv_sem=recv,
            device_id={axis: index}, device_id_type=MESH,
        )
        copy.start()
        sends.append(copy)

    def got(dst, recv):
        pltpu.make_async_remote_copy(
            src_ref=dst, dst_ref=dst, send_sem=send_sem.at[0], recv_sem=recv,
            device_id={"dp": above}, device_id_type=MESH,
        ).wait_recv()

    loads = [
        pltpu.make_async_copy(src, dst, load_sem.at[i])
        for i, (src, dst) in enumerate((
            (gains_in, gains), (gates_in, gates), (inputs_in, inputs), (velocity_in, velocity),
            (lengths_in, lengths), (steps_in, steps),
        ))
    ]
    for load in loads:
        load.start()
    own_rows = pl.ds(pl.multiple_of(x * chunk, 16), chunk)
    keep = pltpu.make_async_copy(w_in.at[0, own_rows], wbuf.at[x, z], local_sem.at[0])
    keep.start()
    small_src[...] = jnp.zeros_like(small_src)
    for load in loads:
        load.wait()
    for to in range(nx):
        for unit in range(nz):
            at = unit * (width // HALVES) + to * chunk
            small_src[to, unit:unit + 1, 0:chunk] = gains[0:1, at:at + chunk]
        for half in range(HALVES):
            at = half * (width // HALVES) + to * chunk
            small_src[to, 16 + half:17 + half, 0:chunk] = gates[0:1, at:at + chunk]

    pl.semaphore_wait(barrier, greeted)

    for d in range(1, nx):
        to = lax.rem(x + d, nx)
        rows = pl.ds(pl.multiple_of(to * chunk, 16), chunk)
        put(w_in.at[0, rows], wbuf.at[x, z], w_sem.at[x], "section", to)
    small_at = pl.ds(pl.multiple_of(x * SMALL_ROWS, 8), SMALL_ROWS)
    for d in range(1, nx):
        to = lax.rem(x + d, nx)
        put(small_src.at[to], small.at[small_at], small_sem.at[x], "section", to)
    small[small_at] = small_src[x]
    keep.wait()

    def wait_piece(s):
        @pl.when(x != s)
        def _():
            got(wbuf.at[s, z], w_sem.at[s])

    def stages(reach):
        return -(-ups // reach)

    def gather_event(s, j):
        reach = GATHER_REACH[s]
        if j == 0:
            wait_piece(s)
        for way, total, sem in ((1, ups, up_sem), (-1, downs, down_sem)):
            gone = j * reach
            if j == stages(reach):
                for q in range(1, total + 1):
                    if q % reach or q >= total:
                        got(wbuf.at[s, lax.rem(z - way * q + nz, nz)], sem.at[s, q - 1])
                continue
            if gone >= total:
                continue
            piece = wbuf.at[s, lax.rem(z - way * gone + nz, nz)]
            if j > 0:
                got(piece, sem.at[s, gone - 1])
            for d in range(min(reach, total - gone), 0, -1):
                put(piece, piece, sem.at[s, gone + d - 1], "dp", lax.rem(z + way * d + nz, nz))

    events = sorted(
        (j + LAG * s, s, j) for s in range(sections) for j in range(stages(GATHER_REACH[s]) + 1)
    )

    def gather_until(key):
        while events and events[0][0] <= key:
            _, s, j = events.pop(0)
            gather_event(s, j)

    def gather_all_of(s):
        while any(event[1] == s for event in events):
            _, section, j = events.pop(0)
            gather_event(section, j)

    gather_until(0)

    lane = lax.broadcasted_iota(jnp.int32, (own, LANES), 1)

    micro, cap = inputs.shape[0], inputs.shape[1]
    slot = lax.broadcasted_iota(jnp.int32, (cap, LANES), 1)
    row = lax.broadcasted_iota(jnp.int32, (cap, LANES), 0)
    first = jnp.zeros((1, 1), jnp.int32)
    factor = jnp.zeros((own, LANES), F32)
    start_block = jnp.zeros((width, LANES), F32)
    target_block = jnp.zeros((width, LANES), F32)
    over_rows = (((0,), (0,)), ((), ()))
    for m in range(micro):
        count = lengths[0:1, m:m + 1]
        chosen = jnp.where((slot - row == first) & (row < count), 1.0, 0.0).astype(BF16)
        start_block += lax.dot_general(inputs[m], chosen, over_rows, preferred_element_type=F32)
        target_block += lax.dot_general(velocity[m], chosen, over_rows, preferred_element_type=F32)
        step = jnp.broadcast_to(steps[0:1, m:m + 1], (own, LANES)).astype(F32)
        weighting = 1.0 / (0.1 + (step + 0.5) / NSTEPS)
        inside = (lane >= first) & (lane < first + count)
        factor = jnp.where(inside, weighting / math.sqrt(LIVE_PER_CLIP * nz), factor)
        first = first + count
    picked[0] = start_block.astype(BF16).reshape(HALVES * nx, chunk, LANES)
    picked[1] = target_block.astype(BF16).reshape(HALVES * nx, chunk, LANES)

    def own_part(which):
        return jnp.concatenate([picked[which, half * nx + x] for half in range(HALVES)], axis=0)

    abuf[0, t] = own_part(0)

    def a_sends(s):
        for d in range(1, nt):
            put(abuf.at[s, t], abuf.at[s, t], a_sem.at[s, t], "tensor", lax.rem(t + d, nt))

    a_sends(0)
    gather_until(1)

    for d in range(1, nx):
        at = lax.rem(x + d, nx)
        got(small.at[pl.ds(pl.multiple_of(at * SMALL_ROWS, 8), SMALL_ROWS)], small_sem.at[at])
    columns = jnp.transpose(small[...])
    wide_lane = lax.broadcasted_iota(jnp.int32, (chunk, LANES), 1)

    def spread_gains(s):
        for unit in range(nz):
            at = s * SMALL_ROWS + unit
            part = jnp.broadcast_to(columns[0:chunk, at:at + 1], (chunk, LANES))
            gainb[s, unit * chunk:(unit + 1) * chunk] = part
            a, b, c = (p.astype(F32) for p in split3(part))
            tail = jnp.where(wide_lane == PARTS_AT + 1, a, 0.0)
            tail = jnp.where(wide_lane == PARTS_AT + 2, b, tail)
            tail = jnp.where(wide_lane == PARTS_AT + 3, c, tail)
            gtail[s, unit * chunk:(unit + 1) * chunk] = tail
        for half in range(HALVES):
            at = s * SMALL_ROWS + 16 + half
            part = jnp.broadcast_to(columns[0:chunk, at:at + 1], (chunk, LANES))
            gateb[s, half * chunk:(half + 1) * chunk] = part

    for s in range(sections):
        spread_gains(s)
        if s < 2:
            gather_until(2)

    factor = jnp.where(lane < LIVE_PER_CLIP, factor, 0.0)

    def key_after(s):
        return stages(2) + LAG * s + 1

    coeff = math.sqrt(2.0 / math.pi)
    state = None
    for s in range(sections):
        if s > 0:
            abuf[s, t] = state
            a_sends(s)
        gather_all_of(s)
        weight = wbuf[s].reshape(deep, width)
        wt[...] = jnp.transpose(weight)
        for d in range(1, nt):
            at = lax.rem(t + d, nt)
            got(abuf.at[s, at], a_sem.at[s, at])
        values = abuf[s].reshape(deep, LANES).astype(F32)
        slice_mean = jnp.sum(values, axis=0, keepdims=True) * (1.0 / deep)
        centred = values - slice_mean
        slice_square = jnp.sum(centred * centred, axis=0, keepdims=True)
        operand = (centred * gainb[s] + gtail[s]).astype(BF16)
        partial = jnp.dot(wt[...], operand, preferred_element_type=F32)
        rounding = partial - partial.astype(BF16).astype(F32)
        all_lane = lax.broadcasted_iota(jnp.int32, (width, LANES), 1)
        partial = jnp.where(
            all_lane == PARTS_AT, pltpu.roll(rounding, LANES - 1, 1), partial
        ).astype(BF16)
        stats = stat_rows(slice_mean, slice_square)
        for to in range(nx):
            for half in range(HALVES):
                at = half * (width // HALVES) + to * chunk
                bsend[s, to, half * chunk:(half + 1) * chunk] = partial[at:at + chunk]
            bsend[s, to, own:own + TAIL] = stats
        for d in range(1, nx):
            to = lax.rem(x + d, nx)
            put(bsend.at[s, to], bbuf.at[s, x], b_sem.at[s, x], "section", to)
        bbuf[s, x] = bsend[s, x]
        gather_until(key_after(s))
        for d in range(1, nx):
            at = lax.rem(x + d, nx)
            got(bbuf.at[s, at], b_sem.at[s, at])
        summed = jnp.zeros((own, LANES), F32)
        means, squares, sums = [], [], []
        for at in range(nx):
            block = bbuf[s, at, 0:own].astype(F32)
            summed += block
            sums.append(
                jnp.sum(jnp.where(lane >= PARTS_AT, block, 0.0), axis=1, keepdims=True)
            )
            one, two = joined(bbuf[s, at, own:own + TAIL])
            means.append(one)
            squares.append(two)
        mean = sum(means[1:], means[0]) * (1.0 / nx)
        square = sum(squares[1:], squares[0])
        for at in range(nx):
            square += deep * (means[at] - mean) * (means[at] - mean)
        inverse = lax.rsqrt(square * (1.0 / model) + EPS)
        total = jnp.where(lane < PARTS_AT, summed, 0.0)
        for at in range(nx):
            total += (means[at] - mean) * sums[at]
        v = total * inverse
        tanh = jnp.tanh(coeff * (v + 0.044715 * v * v * v))
        gelu = 0.5 * v * (1.0 + tanh)
        slope = 0.5 * (1.0 + tanh) + 0.5 * v * (1.0 - tanh * tanh) * coeff * (
            1.0 + 3.0 * 0.044715 * v * v
        )
        gate = gateb[s]
        projb[s] = v
        gelub[s] = gelu
        slopeb[s] = gate * slope
        meanb[s] = mean
        invb[s] = inverse
        ub[s] = jnp.broadcast_to(sum(sums[1:], sums[0]), (own, LANES))
        state = (abuf[s, t].astype(F32) + gate * gelu).astype(BF16)


    target = own_part(1).astype(F32)
    upstream = (factor * (state.astype(F32) - target)).astype(BF16).astype(F32)
    vacc[...] = jnp.zeros_like(vacc)

    def scatter_event(s, turn):
        reach = SCATTER_REACH[s]
        relay = stages(reach) - turn
        mine = dwbuf[s, z].astype(F32) if relay == 0 else None
        for way, total, slots, sem in ((1, ups, rs_up, rsu_sem), (-1, downs, rs_down, rsd_sem)):
            if turn == 0:
                for q in range(total, 0, -1):
                    if q % reach and q > 0 or q == total:
                        d = q - reach * ((q - 1) // reach)
                        to = lax.rem(z + way * d + nz, nz)
                        term = dwbuf.at[s, lax.rem(z + way * q + nz, nz)]
                        put(term, slots.at[s, q - 1], sem.at[s, q - 1], "dp", to)
                continue
            gone = relay * reach
            if gone >= total:
                continue
            children = range(gone + 1, min(gone + reach, total) + 1)
            for q in children:
                got(slots.at[s, q - 1], sem.at[s, q - 1])
            if relay > 0:
                mine = dwbuf[s, lax.rem(z + way * gone + nz, nz)].astype(F32)
            for q in children:
                mine = mine + slots[s, q - 1].astype(F32)
            if relay > 0:
                slots[s, gone] = mine.astype(BF16)
                to = lax.rem(z + way * reach + nz, nz)
                put(slots.at[s, gone], slots.at[s, gone - 1], sem.at[s, gone - 1], "dp", to)
        if relay == 0:
            gw_send[s] = mine.astype(BF16)

            @pl.when(x != s)
            def _():
                put_to(gw_send.at[s], gw_in.at[x], gw_sem.at[x], s)

            @pl.when(x == s)
            def _():
                gw_in[x] = gw_send[s]

    def put_to(src, dst, recv, s):
        pltpu.make_async_remote_copy(
            src_ref=src, dst_ref=dst, send_sem=local_sem.at[1 + s], recv_sem=recv,
            device_id={"section": s}, device_id_type=MESH,
        ).start()

    back = sorted(
        (turn + LAG * (sections - 1 - s), s, turn)
        for s in range(sections) for turn in range(stages(SCATTER_REACH[s]) + 1)
    )

    def scatter_until(key):
        while back and back[0][0] <= key:
            _, s, turn = back.pop(0)
            scatter_event(s, turn)

    for turn, s in enumerate(reversed(range(sections))):
        vacc[0:own] = jnp.where(
            lane == 2 * s, jnp.sum(upstream * gelub[s], axis=1, keepdims=True), vacc[0:own]
        )
        dproj = (upstream * slopeb[s]).astype(BF16)
        exact = dproj.astype(F32)
        first_part = jnp.sum(exact * ub[s], axis=0, keepdims=True)
        second_part = jnp.sum(exact * projb[s], axis=0, keepdims=True)
        dbuf[s, x, 0:own] = dproj
        dbuf[s, x, own:own + TAIL] = stat_rows(first_part, second_part)
        for d in range(1, nx):
            put(dbuf.at[s, x], dbuf.at[s, x], d_sem.at[s, x], "section", lax.rem(x + d, nx))
        if turn > 0:
            scatter_until(LAG * turn - 1)
        mean, inverse = meanb[s], invb[s]
        normed = (
            (abuf[s].reshape(deep, LANES).astype(F32) - mean) * inverse * gainb[s]
        ).astype(BF16)
        for d in range(1, nx):
            at = lax.rem(x + d, nx)
            got(dbuf.at[s, at], d_sem.at[s, at])
        whole = jnp.concatenate(
            [dbuf[s, at, half * chunk:(half + 1) * chunk] for half in range(HALVES) for at in range(nx)],
            axis=0,
        )
        first_sum = jnp.zeros((1, LANES), F32)
        second_sum = jnp.zeros((1, LANES), F32)
        for at in range(nx):
            one, two = joined(dbuf[s, at, own:own + TAIL])
            first_sum += one
            second_sum += two
        product = jnp.dot(wbuf[s].reshape(deep, width), whole, preferred_element_type=F32).astype(BF16)
        stats = stat_rows(first_sum, second_sum)
        for to in range(nt):
            qsend[s, to, 0:own] = product[to * own:(to + 1) * own]
            qsend[s, to, own:own + TAIL] = stats
        for d in range(1, nt):
            to = lax.rem(t + d, nt)
            put(qsend.at[s, to], qbuf.at[s, t], q_sem.at[s, t], "tensor", to)
        qbuf[s, t] = qsend[s, t]
        term = lax.dot_general(
            normed, whole, (((1,), (1,)), ((), ())), preferred_element_type=F32
        )
        dwbuf[s] = term.astype(BF16).reshape(nz, chunk, width)
        scatter_until(LAG * turn)
        for d in range(1, nt):
            at = lax.rem(t + d, nt)
            got(qbuf.at[s, at], q_sem.at[s, at])
        dnormed = jnp.zeros((own, LANES), F32)
        first_moment = jnp.zeros((1, LANES), F32)
        second_moment = jnp.zeros((1, LANES), F32)
        for at in range(nt):
            dnormed += qbuf[s, at, 0:own].astype(F32)
            one, two = joined(qbuf[s, at, own:own + TAIL])
            first_moment += one
            second_moment += two
        xhat = (abuf[s, t].astype(F32) - mean) * inverse
        vacc[0:own] = jnp.where(
            lane == 2 * s + 1, jnp.sum(dnormed * xhat, axis=1, keepdims=True), vacc[0:own]
        )
        if s > 0:
            gain = gainb[s, pl.ds(pl.multiple_of(t * own, 8), own)]
            change = dnormed * gain - first_moment * (1.0 / model) - xhat * (
                second_moment * (1.0 / model)
            )
            upstream = (upstream + inverse * change).astype(BF16).astype(F32)

    v1[member] = jnp.transpose(vacc[...])[0:8]
    for d in range(1, zb):
        to = group * zb + lax.rem(member + d, zb)
        put(v1.at[member], v1.at[member], v1_sem.at[member], "dp", to)
    scatter_until(LAG * (sections - 1) + 1)
    for d in range(1, zb):
        at = lax.rem(member + d, zb)
        got(v1.at[at], v1_sem.at[at])
    v2[group] = v1[0] + v1[1] + v1[2] + v1[3]
    for d in range(1, za):
        to = lax.rem(group + d, za) * zb + member
        put(v2.at[group], v2.at[group], v2_sem.at[group], "dp", to)
    scatter_until(LAG * (sections - 1) + 2)
    for d in range(1, za):
        at = lax.rem(group + d, za)
        got(v2.at[at], v2_sem.at[at])
    full = v2[0]
    for at in range(1, za):
        full = full + v2[at]
    v3[x] = full
    for d in range(1, nx):
        put(v3.at[x], v3.at[x], v3_sem.at[x], "section", lax.rem(x + d, nx))
    scatter_until(LAG * sections + ups)
    for d in range(1, nx):
        at = lax.rem(x + d, nx)
        got(v3.at[at], v3_sem.at[at])
    for at in range(nx):
        tile = v3[at]
        gate_row, gain_row = tile[0:1], tile[1:2]
        for s in range(1, sections):
            gate_row = jnp.where(x == s, tile[2 * s:2 * s + 1], gate_row)
            gain_row = jnp.where(x == s, tile[2 * s + 1:2 * s + 2], gain_row)
        for half in range(HALVES):
            to = half * (width // HALVES) + at * chunk
            gate_out[0:1, to:to + chunk] = gate_row[:, half * chunk:(half + 1) * chunk]
            gain_out[0:1, to:to + chunk] = gain_row[:, half * chunk:(half + 1) * chunk]
    for d in range(1, nx):
        at = lax.rem(x + d, nx)
        got(gw_in.at[at], gw_sem.at[at])
    for at in range(nx):
        gw_out[0, at * chunk:(at + 1) * chunk] = gw_in[at].astype(F32)

    for copy in sends:
        copy.wait_send()
    for s in range(sections):
        @pl.when(x != s)
        def _():
            pltpu.make_async_remote_copy(
                src_ref=gw_send.at[s], dst_ref=gw_in.at[x], send_sem=local_sem.at[1 + s],
                recv_sem=gw_sem.at[x], device_id={"section": s}, device_id_type=MESH,
            ).wait_send()


def local(inputs, velocity, weights, gains, gates, lengths, steps):
    nx, nt, nz = lax.axis_size("section"), lax.axis_size("tensor"), lax.axis_size("dp")
    sections = nx
    width = inputs.shape[2]
    chunk = width // (HALVES * nx)
    own = HALVES * chunk
    deep = nt * own
    ups, downs = nz // 2, nz // 2 - 1
    block = own + TAIL
    sends = (
        2 * (nx - 1) + 2 * sections * (ups + downs) + 2 * sections * (nt - 1)
        + 2 * sections * (nx - 1) + 3 + nz // 4 - 1 + nx - 1
    )
    dma = pltpu.SemaphoreType.DMA
    vmem = pl.BlockSpec(memory_space=pltpu.VMEM)
    anywhere = pl.BlockSpec(memory_space=pl.ANY)
    return pl.pallas_call(
        functools.partial(kernel, nx, nt, nz),
        out_shape=(
            jax.ShapeDtypeStruct((1, nx * chunk, width), F32),
            jax.ShapeDtypeStruct((1, width), F32),
            jax.ShapeDtypeStruct((1, width), F32),
        ),
        in_specs=[anywhere] * 7,
        out_specs=(vmem, vmem, vmem),
        scratch_shapes=[
            pltpu.VMEM(inputs.shape, BF16),
            pltpu.VMEM(velocity.shape, BF16),
            pltpu.VMEM(gains.shape, F32),
            pltpu.VMEM(gates.shape, F32),
            pltpu.VMEM(lengths.shape, jnp.int32),
            pltpu.VMEM(steps.shape, jnp.int32),
            pltpu.VMEM((sections, nz, chunk, width), BF16),
            pltpu.VMEM((width, deep), BF16),
            pltpu.VMEM((nx, SMALL_ROWS, LANES), F32),
            pltpu.VMEM((LANES, LANES), F32),
            pltpu.VMEM((sections, deep, LANES), F32),
            pltpu.VMEM((sections, deep, LANES), F32),
            pltpu.VMEM((sections, own, LANES), F32),
            pltpu.VMEM((2, HALVES * nx, chunk, LANES), BF16),
            pltpu.VMEM((sections, nt, own, LANES), BF16),
            pltpu.VMEM((sections, nx, block, LANES), BF16),
            pltpu.VMEM((sections, nx, block, LANES), BF16),
            pltpu.VMEM((sections, own, LANES), F32),
            pltpu.VMEM((sections, own, LANES), F32),
            pltpu.VMEM((sections, own, LANES), F32),
            pltpu.VMEM((sections, 1, LANES), F32),
            pltpu.VMEM((sections, 1, LANES), F32),
            pltpu.VMEM((sections, own, LANES), F32),
            pltpu.VMEM((sections, nx, block, LANES), BF16),
            pltpu.VMEM((sections, nt, block, LANES), BF16),
            pltpu.VMEM((sections, nt, block, LANES), BF16),
            pltpu.VMEM((sections, nz, chunk, width), BF16),
            pltpu.VMEM((sections, ups, chunk, width), BF16),
            pltpu.VMEM((sections, max(downs, 1), chunk, width), BF16),
            pltpu.VMEM((sections, chunk, width), BF16),
            pltpu.VMEM((nx, chunk, width), BF16),
            pltpu.VMEM((LANES, LANES), F32),
            pltpu.VMEM((4, 8, LANES), F32),
            pltpu.VMEM((max(nz // 4, 1), 8, LANES), F32),
            pltpu.VMEM((nx, 8, LANES), F32),
            dma((sends,)),
            dma((1 + sections,)),
            dma((6,)),
            dma((nx,)),
            dma((nx,)),
            dma((sections, ups)),
            dma((sections, max(downs, 1))),
            dma((sections, nt)),
            dma((sections, nx)),
            dma((sections, nx)),
            dma((sections, nt)),
            dma((sections, ups)),
            dma((sections, max(downs, 1))),
            dma((nx,)),
            dma((4,)),
            dma((max(nz // 4, 1),)),
            dma((nx,)),
        ],
        compiler_params=pltpu.CompilerParams(
            collective_id=0, has_side_effects=True, vmem_limit_bytes=48 * 1024 * 1024
        ),
        name="sections",
    )(weights, inputs, velocity, gains, gates, lengths, steps)


def solution(mesh):
    placed = (
        P(None, "dp", "tensor"),
        P(None, "dp", "tensor"),
        P("section", "dp", "tensor"),
        P("section", None),
        P("section", "tensor"),
        P("dp", None),
        P("dp", None),
    )

    def whole(*args):
        return jax.shard_map(
            local, mesh=mesh, in_specs=placed,
            out_specs=(P("section", "dp", "tensor"), P("section", "tensor"), P("section", "tensor")),
            check_vma=False,
        )(*args)

    return whole
```

```python
import functools
import math

import jax
import jax.numpy as jnp
from jax import lax
from jax.experimental import pallas as pl
from jax.experimental.pallas import tpu as pltpu
from jax.sharding import PartitionSpec as P

MESH = pl.DeviceIdType.MESH
F32 = jnp.float32
BF16 = jnp.bfloat16
NSTEPS = 50
LIVE_PER_CLIP = 100
EPS = 1e-06
LANES = 128
HALVES = 2
SMALL_ROWS = 24
TAIL = 16
PARTS_AT = 124
LAG = 2
GATHER_REACH = (2, 2, 2, 2)
SCATTER_REACH = (2, 2, 2, 2)


def split3(value):
    first = value.astype(BF16)
    rest = value - first.astype(F32)
    second = rest.astype(BF16)
    third = (rest - second.astype(F32)).astype(BF16)
    return first, second, third


def stat_rows(one, two):
    rows = [r.astype(F32) for r in split3(one) + split3(two)]
    rows.append(jnp.zeros((TAIL - 6, LANES), F32))
    return jnp.concatenate(rows, axis=0).astype(BF16)


def joined(block):
    block = block.astype(F32)
    one = block[0:1] + block[1:2] + block[2:3]
    two = block[3:4] + block[4:5] + block[5:6]
    return one, two


def kernel(
    nx, nt, nz,
    w_in, inputs_in, velocity_in, gains_in, gates_in, lengths_in, steps_in,
    gw_out, gain_out, gate_out,
    inputs, velocity, gains, gates, lengths, steps,
    wbuf, wt, small_src, small, gainb, gtail, gateb, picked, abuf, bsend, bbuf,
    projb, gelub, slopeb, meanb, invb, ub, dbuf, qsend, qbuf, dwbuf, rs_up, rs_down,
    gw_send, gw_in, vacc, v1, v2, v3,
    send_sem, local_sem, load_sem, w_sem, small_sem, up_sem, down_sem, a_sem, b_sem, d_sem, q_sem,
    rsu_sem, rsd_sem, gw_sem, v1_sem, v2_sem, v3_sem,
):
    sections = nx
    chunk = gates.shape[1] // (HALVES * nx)
    width = gates.shape[1]
    own = HALVES * chunk
    deep = nt * own
    model = nt * width
    ups, downs = nz // 2, nz // 2 - 1
    zb = 4
    za = nz // zb
    x = lax.axis_index("section")
    t = lax.axis_index("tensor")
    z = lax.axis_index("dp")
    above = lax.rem(z + 1, nz)
    group, member = z // zb, lax.rem(z, zb)

    small[...] = jnp.zeros_like(small)
    barrier = pltpu.get_barrier_semaphore()
    greeted = 0

    def greet(axis, index):
        pl.semaphore_signal(barrier, inc=1, device_id={axis: index}, device_id_type=MESH)

    for d in range(1, nx):
        greet("section", lax.rem(x + d, nx))
        greeted += 1
    far = max(GATHER_REACH + SCATTER_REACH)
    for d in range(1, far + 1):
        greet("dp", lax.rem(z + d, nz))
        greet("dp", lax.rem(z + nz - d, nz))
        greeted += 2
    for d in range(1, nt):
        greet("tensor", lax.rem(t + d, nt))
        greeted += 1

    sends = []

    def put(src, dst, recv, axis, index):
        copy = pltpu.make_async_remote_copy(
            src_ref=src, dst_ref=dst, send_sem=send_sem.at[len(sends)], recv_sem=recv,
            device_id={axis: index}, device_id_type=MESH,
        )
        copy.start()
        sends.append(copy)

    def got(dst, recv):
        pltpu.make_async_remote_copy(
            src_ref=dst, dst_ref=dst, send_sem=send_sem.at[0], recv_sem=recv,
            device_id={"dp": above}, device_id_type=MESH,
        ).wait_recv()

    loads = [
        pltpu.make_async_copy(src, dst, load_sem.at[i])
        for i, (src, dst) in enumerate((
            (gains_in, gains), (gates_in, gates), (inputs_in, inputs), (velocity_in, velocity),
            (lengths_in, lengths), (steps_in, steps),
        ))
    ]
    for load in loads:
        load.start()
    own_rows = pl.ds(pl.multiple_of(x * chunk, 16), chunk)
    keep = pltpu.make_async_copy(w_in.at[0, own_rows], wbuf.at[x, z], local_sem.at[0])
    keep.start()
    small_src[...] = jnp.zeros_like(small_src)
    for load in loads:
        load.wait()
    for to in range(nx):
        for unit in range(nz):
            at = unit * (width // HALVES) + to * chunk
            small_src[to, unit:unit + 1, 0:chunk] = gains[0:1, at:at + chunk]
        for half in range(HALVES):
            at = half * (width // HALVES) + to * chunk
            small_src[to, 16 + half:17 + half, 0:chunk] = gates[0:1, at:at + chunk]

    pl.semaphore_wait(barrier, greeted)

    for d in range(1, nx):
        to = lax.rem(x + d, nx)
        rows = pl.ds(pl.multiple_of(to * chunk, 16), chunk)
        put(w_in.at[0, rows], wbuf.at[x, z], w_sem.at[x], "section", to)
    small_at = pl.ds(pl.multiple_of(x * SMALL_ROWS, 8), SMALL_ROWS)
    for d in range(1, nx):
        to = lax.rem(x + d, nx)
        put(small_src.at[to], small.at[small_at], small_sem.at[x], "section", to)
    small[small_at] = small_src[x]
    keep.wait()

    def wait_piece(s):
        @pl.when(x != s)
        def _():
            got(wbuf.at[s, z], w_sem.at[s])

    def stages(reach):
        return -(-ups // reach)

    def gather_event(s, j):
        reach = GATHER_REACH[s]
        if j == 0:
            wait_piece(s)
        for way, total, sem in ((1, ups, up_sem), (-1, downs, down_sem)):
            gone = j * reach
            if j == stages(reach):
                for q in range(1, total + 1):
                    if q % reach or q >= total:
                        got(wbuf.at[s, lax.rem(z - way * q + nz, nz)], sem.at[s, q - 1])
                continue
            if gone >= total:
                continue
            piece = wbuf.at[s, lax.rem(z - way * gone + nz, nz)]
            if j > 0:
                got(piece, sem.at[s, gone - 1])
            for d in range(min(reach, total - gone), 0, -1):
                put(piece, piece, sem.at[s, gone + d - 1], "dp", lax.rem(z + way * d + nz, nz))

    events = sorted(
        (j + LAG * s, s, j) for s in range(sections) for j in range(stages(GATHER_REACH[s]) + 1)
    )

    def gather_until(key):
        while events and events[0][0] <= key:
            _, s, j = events.pop(0)
            gather_event(s, j)

    def gather_all_of(s):
        while any(event[1] == s for event in events):
            _, section, j = events.pop(0)
            gather_event(section, j)

    gather_until(0)

    lane = lax.broadcasted_iota(jnp.int32, (own, LANES), 1)

    micro, cap = inputs.shape[0], inputs.shape[1]
    slot = lax.broadcasted_iota(jnp.int32, (cap, LANES), 1)
    row = lax.broadcasted_iota(jnp.int32, (cap, LANES), 0)
    first = jnp.zeros((1, 1), jnp.int32)
    factor = jnp.zeros((own, LANES), F32)
    start_block = jnp.zeros((width, LANES), F32)
    target_block = jnp.zeros((width, LANES), F32)
    over_rows = (((0,), (0,)), ((), ()))
    for m in range(micro):
        count = lengths[0:1, m:m + 1]
        chosen = jnp.where((slot - row == first) & (row < count), 1.0, 0.0).astype(BF16)
        start_block += lax.dot_general(inputs[m], chosen, over_rows, preferred_element_type=F32)
        target_block += lax.dot_general(velocity[m], chosen, over_rows, preferred_element_type=F32)
        step = jnp.broadcast_to(steps[0:1, m:m + 1], (own, LANES)).astype(F32)
        weighting = 1.0 / (0.1 + (step + 0.5) / NSTEPS)
        inside = (lane >= first) & (lane < first + count)
        factor = jnp.where(inside, weighting / math.sqrt(LIVE_PER_CLIP * nz), factor)
        first = first + count
    picked[0] = start_block.astype(BF16).reshape(HALVES * nx, chunk, LANES)
    picked[1] = target_block.astype(BF16).reshape(HALVES * nx, chunk, LANES)

    def own_part(which):
        return jnp.concatenate([picked[which, half * nx + x] for half in range(HALVES)], axis=0)

    abuf[0, t] = own_part(0)

    def a_sends(s):
        for d in range(1, nt):
            put(abuf.at[s, t], abuf.at[s, t], a_sem.at[s, t], "tensor", lax.rem(t + d, nt))

    a_sends(0)
    gather_until(1)

    for d in range(1, nx):
        at = lax.rem(x + d, nx)
        got(small.at[pl.ds(pl.multiple_of(at * SMALL_ROWS, 8), SMALL_ROWS)], small_sem.at[at])
    columns = jnp.transpose(small[...])
    wide_lane = lax.broadcasted_iota(jnp.int32, (chunk, LANES), 1)

    def spread_gains(s):
        for unit in range(nz):
            at = s * SMALL_ROWS + unit
            part = jnp.broadcast_to(columns[0:chunk, at:at + 1], (chunk, LANES))
            gainb[s, unit * chunk:(unit + 1) * chunk] = part
            a, b, c = (p.astype(F32) for p in split3(part))
            tail = jnp.where(wide_lane == PARTS_AT + 1, a, 0.0)
            tail = jnp.where(wide_lane == PARTS_AT + 2, b, tail)
            tail = jnp.where(wide_lane == PARTS_AT + 3, c, tail)
            gtail[s, unit * chunk:(unit + 1) * chunk] = tail
        for half in range(HALVES):
            at = s * SMALL_ROWS + 16 + half
            part = jnp.broadcast_to(columns[0:chunk, at:at + 1], (chunk, LANES))
            gateb[s, half * chunk:(half + 1) * chunk] = part

    for s in range(sections):
        spread_gains(s)
        if s < 2:
            gather_until(2)

    factor = jnp.where(lane < LIVE_PER_CLIP, factor, 0.0)

    def key_after(s):
        return stages(2) + LAG * s + 1

    coeff = math.sqrt(2.0 / math.pi)
    state = None
    for s in range(sections):
        if s > 0:
            abuf[s, t] = state
            a_sends(s)
        gather_all_of(s)
        weight = wbuf[s].reshape(deep, width)
        wt[...] = jnp.transpose(weight)
        for d in range(1, nt):
            at = lax.rem(t + d, nt)
            got(abuf.at[s, at], a_sem.at[s, at])
        values = abuf[s].reshape(deep, LANES).astype(F32)
        slice_mean = jnp.sum(values, axis=0, keepdims=True) * (1.0 / deep)
        centred = values - slice_mean
        slice_square = jnp.sum(centred * centred, axis=0, keepdims=True)
        operand = (centred * gainb[s] + gtail[s]).astype(BF16)
        partial = jnp.dot(wt[...], operand, preferred_element_type=F32)
        rounding = partial - partial.astype(BF16).astype(F32)
        all_lane = lax.broadcasted_iota(jnp.int32, (width, LANES), 1)
        partial = jnp.where(
            all_lane == PARTS_AT, pltpu.roll(rounding, LANES - 1, 1), partial
        ).astype(BF16)
        stats = stat_rows(slice_mean, slice_square)
        for to in range(nx):
            for half in range(HALVES):
                at = half * (width // HALVES) + to * chunk
                bsend[s, to, half * chunk:(half + 1) * chunk] = partial[at:at + chunk]
            bsend[s, to, own:own + TAIL] = stats
        for d in range(1, nx):
            to = lax.rem(x + d, nx)
            put(bsend.at[s, to], bbuf.at[s, x], b_sem.at[s, x], "section", to)
        bbuf[s, x] = bsend[s, x]
        gather_until(key_after(s))
        for d in range(1, nx):
            at = lax.rem(x + d, nx)
            got(bbuf.at[s, at], b_sem.at[s, at])
        summed = jnp.zeros((own, LANES), F32)
        means, squares, sums = [], [], []
        for at in range(nx):
            block = bbuf[s, at, 0:own].astype(F32)
            summed += block
            sums.append(
                jnp.sum(jnp.where(lane >= PARTS_AT, block, 0.0), axis=1, keepdims=True)
            )
            one, two = joined(bbuf[s, at, own:own + TAIL])
            means.append(one)
            squares.append(two)
        mean = sum(means[1:], means[0]) * (1.0 / nx)
        square = sum(squares[1:], squares[0])
        for at in range(nx):
            square += deep * (means[at] - mean) * (means[at] - mean)
        inverse = lax.rsqrt(square * (1.0 / model) + EPS)
        total = jnp.where(lane < PARTS_AT, summed, 0.0)
        for at in range(nx):
            total += (means[at] - mean) * sums[at]
        v = total * inverse
        tanh = jnp.tanh(coeff * (v + 0.044715 * v * v * v))
        gelu = 0.5 * v * (1.0 + tanh)
        slope = 0.5 * (1.0 + tanh) + 0.5 * v * (1.0 - tanh * tanh) * coeff * (
            1.0 + 3.0 * 0.044715 * v * v
        )
        gate = gateb[s]
        projb[s] = v
        gelub[s] = gelu
        slopeb[s] = gate * slope
        meanb[s] = mean
        invb[s] = inverse
        ub[s] = jnp.broadcast_to(sum(sums[1:], sums[0]), (own, LANES))
        state = (abuf[s, t].astype(F32) + gate * gelu).astype(BF16)


    target = own_part(1).astype(F32)
    upstream = (factor * (state.astype(F32) - target)).astype(BF16).astype(F32)
    vacc[...] = jnp.zeros_like(vacc)

    def scatter_event(s, turn):
        reach = SCATTER_REACH[s]
        relay = stages(reach) - turn
        mine = dwbuf[s, z].astype(F32) if relay == 0 else None
        for way, total, slots, sem in ((1, ups, rs_up, rsu_sem), (-1, downs, rs_down, rsd_sem)):
            if turn == 0:
                for q in range(total, 0, -1):
                    if q % reach and q > 0 or q == total:
                        d = q - reach * ((q - 1) // reach)
                        to = lax.rem(z + way * d + nz, nz)
                        term = dwbuf.at[s, lax.rem(z + way * q + nz, nz)]
                        put(term, slots.at[s, q - 1], sem.at[s, q - 1], "dp", to)
                continue
            gone = relay * reach
            if gone >= total:
                continue
            children = range(gone + 1, min(gone + reach, total) + 1)
            for q in children:
                got(slots.at[s, q - 1], sem.at[s, q - 1])
            if relay > 0:
                mine = dwbuf[s, lax.rem(z + way * gone + nz, nz)].astype(F32)
            for q in children:
                mine = mine + slots[s, q - 1].astype(F32)
            if relay > 0:
                slots[s, gone] = mine.astype(BF16)
                to = lax.rem(z + way * reach + nz, nz)
                put(slots.at[s, gone], slots.at[s, gone - 1], sem.at[s, gone - 1], "dp", to)
        if relay == 0:
            gw_send[s] = mine.astype(BF16)

            @pl.when(x != s)
            def _():
                put_to(gw_send.at[s], gw_in.at[x], gw_sem.at[x], s)

            @pl.when(x == s)
            def _():
                gw_in[x] = gw_send[s]

    def put_to(src, dst, recv, s):
        pltpu.make_async_remote_copy(
            src_ref=src, dst_ref=dst, send_sem=local_sem.at[1 + s], recv_sem=recv,
            device_id={"section": s}, device_id_type=MESH,
        ).start()

    back = sorted(
        (turn + LAG * (sections - 1 - s), s, turn)
        for s in range(sections) for turn in range(stages(SCATTER_REACH[s]) + 1)
    )

    def scatter_until(key):
        while back and back[0][0] <= key:
            _, s, turn = back.pop(0)
            scatter_event(s, turn)

    for turn, s in enumerate(reversed(range(sections))):
        vacc[0:own] = jnp.where(
            lane == 2 * s, jnp.sum(upstream * gelub[s], axis=1, keepdims=True), vacc[0:own]
        )
        dproj = (upstream * slopeb[s]).astype(BF16)
        exact = dproj.astype(F32)
        first_part = jnp.sum(exact * ub[s], axis=0, keepdims=True)
        second_part = jnp.sum(exact * projb[s], axis=0, keepdims=True)
        dbuf[s, x, 0:own] = dproj
        dbuf[s, x, own:own + TAIL] = stat_rows(first_part, second_part)
        for d in range(1, nx):
            put(dbuf.at[s, x], dbuf.at[s, x], d_sem.at[s, x], "section", lax.rem(x + d, nx))
        if turn > 0:
            scatter_until(LAG * turn - 1)
        mean, inverse = meanb[s], invb[s]
        normed = (
            (abuf[s].reshape(deep, LANES).astype(F32) - mean) * inverse * gainb[s]
        ).astype(BF16)
        for d in range(1, nx):
            at = lax.rem(x + d, nx)
            got(dbuf.at[s, at], d_sem.at[s, at])
        whole = jnp.concatenate(
            [dbuf[s, at, half * chunk:(half + 1) * chunk] for half in range(HALVES) for at in range(nx)],
            axis=0,
        )
        first_sum = jnp.zeros((1, LANES), F32)
        second_sum = jnp.zeros((1, LANES), F32)
        for at in range(nx):
            one, two = joined(dbuf[s, at, own:own + TAIL])
            first_sum += one
            second_sum += two
        product = jnp.dot(wbuf[s].reshape(deep, width), whole, preferred_element_type=F32).astype(BF16)
        stats = stat_rows(first_sum, second_sum)
        for to in range(nt):
            qsend[s, to, 0:own] = product[to * own:(to + 1) * own]
            qsend[s, to, own:own + TAIL] = stats
        for d in range(1, nt):
            to = lax.rem(t + d, nt)
            put(qsend.at[s, to], qbuf.at[s, t], q_sem.at[s, t], "tensor", to)
        qbuf[s, t] = qsend[s, t]
        term = lax.dot_general(
            normed, whole, (((1,), (1,)), ((), ())), preferred_element_type=F32
        )
        dwbuf[s] = term.astype(BF16).reshape(nz, chunk, width)
        scatter_until(LAG * turn)
        for d in range(1, nt):
            at = lax.rem(t + d, nt)
            got(qbuf.at[s, at], q_sem.at[s, at])
        dnormed = jnp.zeros((own, LANES), F32)
        first_moment = jnp.zeros((1, LANES), F32)
        second_moment = jnp.zeros((1, LANES), F32)
        for at in range(nt):
            dnormed += qbuf[s, at, 0:own].astype(F32)
            one, two = joined(qbuf[s, at, own:own + TAIL])
            first_moment += one
            second_moment += two
        xhat = (abuf[s, t].astype(F32) - mean) * inverse
        vacc[0:own] = jnp.where(
            lane == 2 * s + 1, jnp.sum(dnormed * xhat, axis=1, keepdims=True), vacc[0:own]
        )
        if s > 0:
            gain = gainb[s, pl.ds(pl.multiple_of(t * own, 8), own)]
            change = dnormed * gain - first_moment * (1.0 / model) - xhat * (
                second_moment * (1.0 / model)
            )
            upstream = (upstream + inverse * change).astype(BF16).astype(F32)

    v1[member] = jnp.transpose(vacc[...])[0:8]
    for d in range(1, zb):
        to = group * zb + lax.rem(member + d, zb)
        put(v1.at[member], v1.at[member], v1_sem.at[member], "dp", to)
    scatter_until(LAG * (sections - 1) + 1)
    for d in range(1, zb):
        at = lax.rem(member + d, zb)
        got(v1.at[at], v1_sem.at[at])
    v2[group] = v1[0] + v1[1] + v1[2] + v1[3]
    for d in range(1, za):
        to = lax.rem(group + d, za) * zb + member
        put(v2.at[group], v2.at[group], v2_sem.at[group], "dp", to)
    scatter_until(LAG * (sections - 1) + 2)
    for d in range(1, za):
        at = lax.rem(group + d, za)
        got(v2.at[at], v2_sem.at[at])
    full = v2[0]
    for at in range(1, za):
        full = full + v2[at]
    v3[x] = full
    for d in range(1, nx):
        put(v3.at[x], v3.at[x], v3_sem.at[x], "section", lax.rem(x + d, nx))
    scatter_until(LAG * sections + ups)
    for d in range(1, nx):
        at = lax.rem(x + d, nx)
        got(v3.at[at], v3_sem.at[at])
    for at in range(nx):
        tile = v3[at]
        gate_row, gain_row = tile[0:1], tile[1:2]
        for s in range(1, sections):
            gate_row = jnp.where(x == s, tile[2 * s:2 * s + 1], gate_row)
            gain_row = jnp.where(x == s, tile[2 * s + 1:2 * s + 2], gain_row)
        for half in range(HALVES):
            to = half * (width // HALVES) + at * chunk
            gate_out[0:1, to:to + chunk] = gate_row[:, half * chunk:(half + 1) * chunk]
            gain_out[0:1, to:to + chunk] = gain_row[:, half * chunk:(half + 1) * chunk]
    for d in range(1, nx):
        at = lax.rem(x + d, nx)
        got(gw_in.at[at], gw_sem.at[at])
    for at in range(nx):
        gw_out[0, at * chunk:(at + 1) * chunk] = gw_in[at].astype(F32)

    for copy in sends:
        copy.wait_send()
    for s in range(sections):
        @pl.when(x != s)
        def _():
            pltpu.make_async_remote_copy(
                src_ref=gw_send.at[s], dst_ref=gw_in.at[x], send_sem=local_sem.at[1 + s],
                recv_sem=gw_sem.at[x], device_id={"section": s}, device_id_type=MESH,
            ).wait_send()


def local(inputs, velocity, weights, gains, gates, lengths, steps):
    nx, nt, nz = lax.axis_size("section"), lax.axis_size("tensor"), lax.axis_size("dp")
    sections = nx
    width = inputs.shape[2]
    chunk = width // (HALVES * nx)
    own = HALVES * chunk
    deep = nt * own
    ups, downs = nz // 2, nz // 2 - 1
    block = own + TAIL
    sends = (
        2 * (nx - 1) + 2 * sections * (ups + downs) + 2 * sections * (nt - 1)
        + 2 * sections * (nx - 1) + 3 + nz // 4 - 1 + nx - 1
    )
    dma = pltpu.SemaphoreType.DMA
    vmem = pl.BlockSpec(memory_space=pltpu.VMEM)
    anywhere = pl.BlockSpec(memory_space=pltpu.HBM)
    return pl.pallas_call(
        functools.partial(kernel, nx, nt, nz),
        out_shape=(
            jax.ShapeDtypeStruct((1, nx * chunk, width), F32),
            jax.ShapeDtypeStruct((1, width), F32),
            jax.ShapeDtypeStruct((1, width), F32),
        ),
        in_specs=[anywhere] * 7,
        out_specs=(vmem, vmem, vmem),
        scratch_shapes=[
            pltpu.VMEM(inputs.shape, BF16),
            pltpu.VMEM(velocity.shape, BF16),
            pltpu.VMEM(gains.shape, F32),
            pltpu.VMEM(gates.shape, F32),
            pltpu.VMEM(lengths.shape, jnp.int32),
            pltpu.VMEM(steps.shape, jnp.int32),
            pltpu.VMEM((sections, nz, chunk, width), BF16),
            pltpu.VMEM((width, deep), BF16),
            pltpu.VMEM((nx, SMALL_ROWS, LANES), F32),
            pltpu.VMEM((LANES, LANES), F32),
            pltpu.VMEM((sections, deep, LANES), F32),
            pltpu.VMEM((sections, deep, LANES), F32),
            pltpu.VMEM((sections, own, LANES), F32),
            pltpu.VMEM((2, HALVES * nx, chunk, LANES), BF16),
            pltpu.VMEM((sections, nt, own, LANES), BF16),
            pltpu.VMEM((sections, nx, block, LANES), BF16),
            pltpu.VMEM((sections, nx, block, LANES), BF16),
            pltpu.VMEM((sections, own, LANES), F32),
            pltpu.VMEM((sections, own, LANES), F32),
            pltpu.VMEM((sections, own, LANES), F32),
            pltpu.VMEM((sections, 1, LANES), F32),
            pltpu.VMEM((sections, 1, LANES), F32),
            pltpu.VMEM((sections, own, LANES), F32),
            pltpu.VMEM((sections, nx, block, LANES), BF16),
            pltpu.VMEM((sections, nt, block, LANES), BF16),
            pltpu.VMEM((sections, nt, block, LANES), BF16),
            pltpu.VMEM((sections, nz, chunk, width), BF16),
            pltpu.VMEM((sections, ups, chunk, width), BF16),
            pltpu.VMEM((sections, max(downs, 1), chunk, width), BF16),
            pltpu.VMEM((sections, chunk, width), BF16),
            pltpu.VMEM((nx, chunk, width), BF16),
            pltpu.VMEM((LANES, LANES), F32),
            pltpu.VMEM((4, 8, LANES), F32),
            pltpu.VMEM((max(nz // 4, 1), 8, LANES), F32),
            pltpu.VMEM((nx, 8, LANES), F32),
            dma((sends,)),
            dma((1 + sections,)),
            dma((6,)),
            dma((nx,)),
            dma((nx,)),
            dma((sections, ups)),
            dma((sections, max(downs, 1))),
            dma((sections, nt)),
            dma((sections, nx)),
            dma((sections, nx)),
            dma((sections, nt)),
            dma((sections, ups)),
            dma((sections, max(downs, 1))),
            dma((nx,)),
            dma((4,)),
            dma((max(nz // 4, 1),)),
            dma((nx,)),
        ],
        compiler_params=pltpu.CompilerParams(
            collective_id=0, has_side_effects=True, vmem_limit_bytes=64 * 1024 * 1024
        ),
        name="sections",
    )(weights, inputs, velocity, gains, gates, lengths, steps)


def solution(mesh):
    placed = (
        P(None, "dp", "tensor"),
        P(None, "dp", "tensor"),
        P("section", "dp", "tensor"),
        P("section", None),
        P("section", "tensor"),
        P("dp", None),
        P("dp", None),
    )

    def whole(*args):
        return jax.shard_map(
            local, mesh=mesh, in_specs=placed,
            out_specs=(P("section", "dp", "tensor"), P("section", "tensor"), P("section", "tensor")),
            check_vma=False,
        )(*args)

    return whole
```

```python
import functools
import math

import jax
import jax.numpy as jnp
from jax import lax
from jax.experimental import pallas as pl
from jax.experimental.pallas import tpu as pltpu
from jax.sharding import PartitionSpec as P

MESH = pl.DeviceIdType.MESH
F32 = jnp.float32
BF16 = jnp.bfloat16
NSTEPS = 50
LIVE_PER_CLIP = 100
EPS = 1e-06
LANES = 128
HALVES = 2
SMALL_ROWS = 24
TAIL = 16
PARTS_AT = 124
GATHER_REACH = (2, 2, 1, 1)
GATHER_START = (0, 2, 0, 2)
SCATTER_REACH = (2, 2, 2, 2)
SCATTER_START = (6, 4, 2, 0)


def split3(value):
    first = value.astype(BF16)
    rest = value - first.astype(F32)
    second = rest.astype(BF16)
    third = (rest - second.astype(F32)).astype(BF16)
    return first, second, third


def stat_rows(one, two):
    rows = [r.astype(F32) for r in split3(one) + split3(two)]
    rows.append(jnp.zeros((TAIL - 6, LANES), F32))
    return jnp.concatenate(rows, axis=0).astype(BF16)


def joined(block):
    block = block.astype(F32)
    one = block[0:1] + block[1:2] + block[2:3]
    two = block[3:4] + block[4:5] + block[5:6]
    return one, two


def kernel(
    nx, nt, nz,
    w_in, inputs_in, velocity_in, gains_in, gates_in, lengths_in, steps_in,
    gw_part, row_part,
    inputs, velocity, gains, gates, lengths, steps,
    wbuf, wt, small_src, small, gainb, gtail, gateb, picked, abuf, bsend, bbuf,
    projb, gelub, slopeb, meanb, invb, ub, dbuf, qsend, qbuf, dwbuf, rs_up, rs_down,
    gw_send, gw_in, vacc, v1, v2, v3,
    send_sem, local_sem, load_sem, w_sem, small_sem, up_sem, down_sem, a_sem, b_sem, d_sem, q_sem,
    rsu_sem, rsd_sem, gw_sem, v1_sem, v2_sem, v3_sem,
):
    sections = nx
    chunk = gates.shape[1] // (HALVES * nx)
    width = gates.shape[1]
    own = HALVES * chunk
    deep = nt * own
    model = nt * width
    ups, downs = nz // 2, nz // 2 - 1
    zb = 4
    za = nz // zb
    x = lax.axis_index("section")
    t = lax.axis_index("tensor")
    z = lax.axis_index("dp")
    above = lax.rem(z + 1, nz)
    group, member = z // zb, lax.rem(z, zb)

    small[...] = jnp.zeros_like(small)
    barrier = pltpu.get_barrier_semaphore()
    greeted = 0

    def greet(axis, index):
        pl.semaphore_signal(barrier, inc=1, device_id={axis: index}, device_id_type=MESH)

    for d in range(1, nx):
        greet("section", lax.rem(x + d, nx))
        greeted += 1
    far = max(GATHER_REACH + SCATTER_REACH)
    for d in range(1, far + 1):
        greet("dp", lax.rem(z + d, nz))
        greet("dp", lax.rem(z + nz - d, nz))
        greeted += 2
    for d in range(1, nt):
        greet("tensor", lax.rem(t + d, nt))
        greeted += 1

    far_x = sorted(range(1, nx), key=lambda d: -min(d, nx - d))
    far_t = sorted(range(1, nt), key=lambda d: -min(d, nt - d))
    sends = []

    def put(src, dst, recv, axis, index):
        copy = pltpu.make_async_remote_copy(
            src_ref=src, dst_ref=dst, send_sem=send_sem.at[len(sends)], recv_sem=recv,
            device_id={axis: index}, device_id_type=MESH,
        )
        copy.start()
        sends.append(copy)

    def got(dst, recv):
        pltpu.make_async_remote_copy(
            src_ref=dst, dst_ref=dst, send_sem=send_sem.at[0], recv_sem=recv,
            device_id={"dp": above}, device_id_type=MESH,
        ).wait_recv()

    loads = [
        pltpu.make_async_copy(src, dst, load_sem.at[i])
        for i, (src, dst) in enumerate((
            (gains_in, gains), (gates_in, gates), (inputs_in, inputs), (velocity_in, velocity),
            (lengths_in, lengths), (steps_in, steps),
        ))
    ]
    for load in loads:
        load.start()
    own_rows = pl.ds(pl.multiple_of(x * chunk, 16), chunk)
    keep = pltpu.make_async_copy(w_in.at[0, own_rows], wbuf.at[x, z], local_sem.at[0])
    keep.start()
    small_src[...] = jnp.zeros_like(small_src)
    for load in loads:
        load.wait()
    for to in range(nx):
        for unit in range(nz):
            at = unit * (width // HALVES) + to * chunk
            small_src[to, unit:unit + 1, 0:chunk] = gains[0:1, at:at + chunk]
        for half in range(HALVES):
            at = half * (width // HALVES) + to * chunk
            small_src[to, 16 + half:17 + half, 0:chunk] = gates[0:1, at:at + chunk]

    pl.semaphore_wait(barrier, greeted)

    for d in far_x:
        to = lax.rem(x + d, nx)
        rows = pl.ds(pl.multiple_of(to * chunk, 16), chunk)
        put(w_in.at[0, rows], wbuf.at[x, z], w_sem.at[x], "section", to)
    small_at = pl.ds(pl.multiple_of(x * SMALL_ROWS, 8), SMALL_ROWS)
    for d in range(1, nx):
        to = lax.rem(x + d, nx)
        put(small_src.at[to], small.at[small_at], small_sem.at[x], "section", to)
    small[small_at] = small_src[x]
    keep.wait()

    def wait_piece(s):
        @pl.when(x != s)
        def _():
            got(wbuf.at[s, z], w_sem.at[s])

    def stages(reach):
        return -(-ups // reach)

    def gather_event(s, j):
        reach = GATHER_REACH[s]
        if j == 0:
            wait_piece(s)
        for way, total, sem in ((1, ups, up_sem), (-1, downs, down_sem)):
            gone = j * reach
            if j == stages(reach):
                for q in range(1, total + 1):
                    if q % reach or q >= total:
                        got(wbuf.at[s, lax.rem(z - way * q + nz, nz)], sem.at[s, q - 1])
                continue
            if gone >= total:
                continue
            piece = wbuf.at[s, lax.rem(z - way * gone + nz, nz)]
            if j > 0:
                got(piece, sem.at[s, gone - 1])
            for d in range(min(reach, total - gone), 0, -1):
                put(piece, piece, sem.at[s, gone + d - 1], "dp", lax.rem(z + way * d + nz, nz))

    events = sorted(
        (j + GATHER_START[s], s, j) for s in range(sections) for j in range(stages(GATHER_REACH[s]) + 1)
    )

    def gather_until(key):
        while events and events[0][0] <= key:
            _, s, j = events.pop(0)
            gather_event(s, j)

    def gather_all_of(s):
        while any(event[1] == s for event in events):
            _, section, j = events.pop(0)
            gather_event(section, j)

    gather_until(0)

    lane = lax.broadcasted_iota(jnp.int32, (own, LANES), 1)

    micro, cap = inputs.shape[0], inputs.shape[1]
    slot = lax.broadcasted_iota(jnp.int32, (cap, LANES), 1)
    row = lax.broadcasted_iota(jnp.int32, (cap, LANES), 0)
    first = jnp.zeros((1, 1), jnp.int32)
    factor = jnp.zeros((own, LANES), F32)
    start_block = jnp.zeros((width, LANES), F32)
    target_block = jnp.zeros((width, LANES), F32)
    over_rows = (((0,), (0,)), ((), ()))
    for m in range(micro):
        count = lengths[0:1, m:m + 1]
        chosen = jnp.where((slot - row == first) & (row < count), 1.0, 0.0).astype(BF16)
        start_block += lax.dot_general(inputs[m], chosen, over_rows, preferred_element_type=F32)
        target_block += lax.dot_general(velocity[m], chosen, over_rows, preferred_element_type=F32)
        step = jnp.broadcast_to(steps[0:1, m:m + 1], (own, LANES)).astype(F32)
        weighting = 1.0 / (0.1 + (step + 0.5) / NSTEPS)
        inside = (lane >= first) & (lane < first + count)
        factor = jnp.where(inside, weighting / math.sqrt(LIVE_PER_CLIP * nz), factor)
        first = first + count
    picked[0] = start_block.astype(BF16).reshape(HALVES * nx, chunk, LANES)
    picked[1] = target_block.astype(BF16).reshape(HALVES * nx, chunk, LANES)

    def own_part(which):
        return jnp.concatenate([picked[which, half * nx + x] for half in range(HALVES)], axis=0)

    abuf[0, t] = own_part(0)

    def a_sends(s):
        for d in far_t:
            put(abuf.at[s, t], abuf.at[s, t], a_sem.at[s, t], "tensor", lax.rem(t + d, nt))

    a_sends(0)
    gather_until(1)

    for d in range(1, nx):
        at = lax.rem(x + d, nx)
        got(small.at[pl.ds(pl.multiple_of(at * SMALL_ROWS, 8), SMALL_ROWS)], small_sem.at[at])
    columns = jnp.transpose(small[...])
    wide_lane = lax.broadcasted_iota(jnp.int32, (chunk, LANES), 1)

    def spread_gains(s):
        for unit in range(nz):
            at = s * SMALL_ROWS + unit
            part = jnp.broadcast_to(columns[0:chunk, at:at + 1], (chunk, LANES))
            gainb[s, unit * chunk:(unit + 1) * chunk] = part
            a, b, c = (p.astype(F32) for p in split3(part))
            tail = jnp.where(wide_lane == PARTS_AT + 1, a, 0.0)
            tail = jnp.where(wide_lane == PARTS_AT + 2, b, tail)
            tail = jnp.where(wide_lane == PARTS_AT + 3, c, tail)
            gtail[s, unit * chunk:(unit + 1) * chunk] = tail
        for half in range(HALVES):
            at = s * SMALL_ROWS + 16 + half
            part = jnp.broadcast_to(columns[0:chunk, at:at + 1], (chunk, LANES))
            gateb[s, half * chunk:(half + 1) * chunk] = part

    for s in range(sections):
        spread_gains(s)
        if s < 2:
            gather_until(2 + s)

    factor = jnp.where(lane < LIVE_PER_CLIP, factor, 0.0)

    def key_after(s):
        return stages(GATHER_REACH[0]) + 2 * s + 1

    coeff = math.sqrt(2.0 / math.pi)
    state = None
    for s in range(sections):
        if s > 0:
            abuf[s, t] = state
            a_sends(s)
        gather_all_of(s)
        weight = wbuf[s].reshape(deep, width)
        wt[...] = jnp.transpose(weight)
        for d in range(1, nt):
            at = lax.rem(t + d, nt)
            got(abuf.at[s, at], a_sem.at[s, at])
        values = abuf[s].reshape(deep, LANES).astype(F32)
        slice_mean = jnp.sum(values, axis=0, keepdims=True) * (1.0 / deep)
        centred = values - slice_mean
        slice_square = jnp.sum(centred * centred, axis=0, keepdims=True)
        operand = (centred * gainb[s] + gtail[s]).astype(BF16)
        partial = jnp.dot(wt[...], operand, preferred_element_type=F32)
        rounding = partial - partial.astype(BF16).astype(F32)
        all_lane = lax.broadcasted_iota(jnp.int32, (width, LANES), 1)
        partial = jnp.where(
            all_lane == PARTS_AT, pltpu.roll(rounding, LANES - 1, 1), partial
        ).astype(BF16)
        stats = stat_rows(slice_mean, slice_square)
        for to in range(nx):
            for half in range(HALVES):
                at = half * (width // HALVES) + to * chunk
                bsend[s, to, half * chunk:(half + 1) * chunk] = partial[at:at + chunk]
            bsend[s, to, own:own + TAIL] = stats
        for d in far_x:
            to = lax.rem(x + d, nx)
            put(bsend.at[s, to], bbuf.at[s, x], b_sem.at[s, x], "section", to)
        bbuf[s, x] = bsend[s, x]
        gather_until(key_after(s))
        for d in range(1, nx):
            at = lax.rem(x + d, nx)
            got(bbuf.at[s, at], b_sem.at[s, at])
        summed = jnp.zeros((own, LANES), F32)
        means, squares, sums = [], [], []
        for at in range(nx):
            block = bbuf[s, at, 0:own].astype(F32)
            summed += block
            sums.append(
                jnp.sum(jnp.where(lane >= PARTS_AT, block, 0.0), axis=1, keepdims=True)
            )
            one, two = joined(bbuf[s, at, own:own + TAIL])
            means.append(one)
            squares.append(two)
        mean = sum(means[1:], means[0]) * (1.0 / nx)
        square = sum(squares[1:], squares[0])
        for at in range(nx):
            square += deep * (means[at] - mean) * (means[at] - mean)
        inverse = lax.rsqrt(square * (1.0 / model) + EPS)
        total = jnp.where(lane < PARTS_AT, summed, 0.0)
        for at in range(nx):
            total += (means[at] - mean) * sums[at]
        v = total * inverse
        tanh = jnp.tanh(coeff * (v + 0.044715 * v * v * v))
        gelu = 0.5 * v * (1.0 + tanh)
        slope = 0.5 * (1.0 + tanh) + 0.5 * v * (1.0 - tanh * tanh) * coeff * (
            1.0 + 3.0 * 0.044715 * v * v
        )
        gate = gateb[s]
        projb[s] = v
        gelub[s] = gelu
        slopeb[s] = gate * slope
        meanb[s] = mean
        invb[s] = inverse
        ub[s] = jnp.broadcast_to(sum(sums[1:], sums[0]), (own, LANES))
        state = (abuf[s, t].astype(F32) + gate * gelu).astype(BF16)


    target = own_part(1).astype(F32)
    upstream = (factor * (state.astype(F32) - target)).astype(BF16).astype(F32)
    vacc[...] = jnp.zeros_like(vacc)

    def scatter_event(s, turn):
        reach = SCATTER_REACH[s]
        relay = stages(reach) - turn
        mine = dwbuf[s, z].astype(F32) if relay == 0 else None
        for way, total, slots, sem in ((1, ups, rs_up, rsu_sem), (-1, downs, rs_down, rsd_sem)):
            if turn == 0:
                for q in range(total, 0, -1):
                    if q % reach and q > 0 or q == total:
                        d = q - reach * ((q - 1) // reach)
                        to = lax.rem(z + way * d + nz, nz)
                        term = dwbuf.at[s, lax.rem(z + way * q + nz, nz)]
                        put(term, slots.at[s, q - 1], sem.at[s, q - 1], "dp", to)
                continue
            gone = relay * reach
            if gone >= total:
                continue
            children = range(gone + 1, min(gone + reach, total) + 1)
            for q in children:
                got(slots.at[s, q - 1], sem.at[s, q - 1])
            if relay > 0:
                mine = dwbuf[s, lax.rem(z + way * gone + nz, nz)].astype(F32)
            for q in children:
                mine = mine + slots[s, q - 1].astype(F32)
            if relay > 0:
                slots[s, gone] = mine.astype(BF16)
                to = lax.rem(z + way * reach + nz, nz)
                put(slots.at[s, gone], slots.at[s, gone - 1], sem.at[s, gone - 1], "dp", to)
        if relay == 0:
            gw_send[s] = mine.astype(BF16)

            @pl.when(x != s)
            def _():
                put_to(gw_send.at[s], gw_in.at[x], gw_sem.at[x], s)

            @pl.when(x == s)
            def _():
                gw_in[x] = gw_send[s]

    def put_to(src, dst, recv, s):
        pltpu.make_async_remote_copy(
            src_ref=src, dst_ref=dst, send_sem=local_sem.at[1 + s], recv_sem=recv,
            device_id={"section": s}, device_id_type=MESH,
        ).start()

    back = sorted(
        (turn + SCATTER_START[s], s, turn)
        for s in range(sections) for turn in range(stages(SCATTER_REACH[s]) + 1)
    )

    def scatter_until(key):
        while back and back[0][0] <= key:
            _, s, turn = back.pop(0)
            scatter_event(s, turn)

    for turn, s in enumerate(reversed(range(sections))):
        vacc[0:own] = jnp.where(
            lane == 2 * s, jnp.sum(upstream * gelub[s], axis=1, keepdims=True), vacc[0:own]
        )
        dproj = (upstream * slopeb[s]).astype(BF16)
        exact = dproj.astype(F32)
        first_part = jnp.sum(exact * ub[s], axis=0, keepdims=True)
        second_part = jnp.sum(exact * projb[s], axis=0, keepdims=True)
        dbuf[s, x, 0:own] = dproj
        dbuf[s, x, own:own + TAIL] = stat_rows(first_part, second_part)
        for d in far_x:
            put(dbuf.at[s, x], dbuf.at[s, x], d_sem.at[s, x], "section", lax.rem(x + d, nx))
        if turn > 0:
            scatter_until(2 * turn - 1)
        mean, inverse = meanb[s], invb[s]
        normed = (
            (abuf[s].reshape(deep, LANES).astype(F32) - mean) * inverse * gainb[s]
        ).astype(BF16)
        for d in range(1, nx):
            at = lax.rem(x + d, nx)
            got(dbuf.at[s, at], d_sem.at[s, at])
        whole = jnp.concatenate(
            [dbuf[s, at, half * chunk:(half + 1) * chunk] for half in range(HALVES) for at in range(nx)],
            axis=0,
        )
        first_sum = jnp.zeros((1, LANES), F32)
        second_sum = jnp.zeros((1, LANES), F32)
        for at in range(nx):
            one, two = joined(dbuf[s, at, own:own + TAIL])
            first_sum += one
            second_sum += two
        product = jnp.dot(wbuf[s].reshape(deep, width), whole, preferred_element_type=F32).astype(BF16)
        stats = stat_rows(first_sum, second_sum)
        for to in range(nt):
            qsend[s, to, 0:own] = product[to * own:(to + 1) * own]
            qsend[s, to, own:own + TAIL] = stats
        for d in far_t:
            to = lax.rem(t + d, nt)
            put(qsend.at[s, to], qbuf.at[s, t], q_sem.at[s, t], "tensor", to)
        qbuf[s, t] = qsend[s, t]
        term = lax.dot_general(
            normed, whole, (((1,), (1,)), ((), ())), preferred_element_type=F32
        )
        dwbuf[s] = term.astype(BF16).reshape(nz, chunk, width)
        scatter_until(2 * turn)
        for d in range(1, nt):
            at = lax.rem(t + d, nt)
            got(qbuf.at[s, at], q_sem.at[s, at])
        dnormed = jnp.zeros((own, LANES), F32)
        first_moment = jnp.zeros((1, LANES), F32)
        second_moment = jnp.zeros((1, LANES), F32)
        for at in range(nt):
            dnormed += qbuf[s, at, 0:own].astype(F32)
            one, two = joined(qbuf[s, at, own:own + TAIL])
            first_moment += one
            second_moment += two
        xhat = (abuf[s, t].astype(F32) - mean) * inverse
        vacc[0:own] = jnp.where(
            lane == 2 * s + 1, jnp.sum(dnormed * xhat, axis=1, keepdims=True), vacc[0:own]
        )
        if s > 0:
            gain = gainb[s, pl.ds(pl.multiple_of(t * own, 8), own)]
            change = dnormed * gain - first_moment * (1.0 / model) - xhat * (
                second_moment * (1.0 / model)
            )
            upstream = (upstream + inverse * change).astype(BF16).astype(F32)

    v1[member] = jnp.transpose(vacc[...])[0:8]
    for d in range(1, zb):
        to = group * zb + lax.rem(member + d, zb)
        put(v1.at[member], v1.at[member], v1_sem.at[member], "dp", to)
    scatter_until(SCATTER_START[0] + 1)
    for d in range(1, zb):
        at = lax.rem(member + d, zb)
        got(v1.at[at], v1_sem.at[at])
    v2[group] = v1[0] + v1[1] + v1[2] + v1[3]
    for d in range(1, za):
        to = lax.rem(group + d, za) * zb + member
        put(v2.at[group], v2.at[group], v2_sem.at[group], "dp", to)
    scatter_until(SCATTER_START[0] + stages(SCATTER_REACH[0]) - 1)
    for d in range(1, za):
        at = lax.rem(group + d, za)
        got(v2.at[at], v2_sem.at[at])
    full = v2[0]
    for at in range(1, za):
        full = full + v2[at]
    v3[x] = full
    for d in far_x:
        put(v3.at[x], v3.at[x], v3_sem.at[x], "section", lax.rem(x + d, nx))
    while back:
        _, s, turn = back.pop(0)
        scatter_event(s, turn)
    for d in range(1, nx):
        at = lax.rem(x + d, nx)
        got(v3.at[at], v3_sem.at[at])
    for at in range(nx):
        tile = v3[at]
        gate_row, gain_row = tile[0:1], tile[1:2]
        for s in range(1, sections):
            gate_row = jnp.where(x == s, tile[2 * s:2 * s + 1], gate_row)
            gain_row = jnp.where(x == s, tile[2 * s + 1:2 * s + 2], gain_row)
        for half in range(HALVES):
            to = half * (width // HALVES) + at * chunk
            row_part[0:1, to:to + chunk] = gate_row[:, half * chunk:(half + 1) * chunk]
            row_part[1:2, to:to + chunk] = gain_row[:, half * chunk:(half + 1) * chunk]
    for d in range(1, nx):
        at = lax.rem(x + d, nx)
        got(gw_in.at[at], gw_sem.at[at])
    gw_part[...] = gw_in[...]

    for copy in sends:
        copy.wait_send()
    for s in range(sections):
        @pl.when(x != s)
        def _():
            pltpu.make_async_remote_copy(
                src_ref=gw_send.at[s], dst_ref=gw_in.at[x], send_sem=local_sem.at[1 + s],
                recv_sem=gw_sem.at[x], device_id={"section": s}, device_id_type=MESH,
            ).wait_send()


def results(parts, rows, weight_out, gain_out, gate_out):
    chunk = parts.shape[1]
    for at in range(parts.shape[0]):
        weight_out[0, at * chunk:(at + 1) * chunk] = parts[at].astype(F32)
    gate_out[...] = rows[0:1]
    gain_out[...] = rows[1:2]


def local(inputs, velocity, weights, gains, gates, lengths, steps):
    nx, nt, nz = lax.axis_size("section"), lax.axis_size("tensor"), lax.axis_size("dp")
    sections = nx
    width = inputs.shape[2]
    chunk = width // (HALVES * nx)
    own = HALVES * chunk
    deep = nt * own
    ups, downs = nz // 2, nz // 2 - 1
    block = own + TAIL
    sends = (
        2 * (nx - 1) + 2 * sections * (ups + downs) + 2 * sections * (nt - 1)
        + 2 * sections * (nx - 1) + 3 + nz // 4 - 1 + nx - 1
    )
    dma = pltpu.SemaphoreType.DMA
    vmem = pl.BlockSpec(memory_space=pltpu.VMEM)
    anywhere = pl.BlockSpec(memory_space=pltpu.HBM)
    parts, rows = pl.pallas_call(
        functools.partial(kernel, nx, nt, nz),
        out_shape=(
            jax.ShapeDtypeStruct((nx, chunk, width), BF16),
            jax.ShapeDtypeStruct((2, width), F32),
        ),
        in_specs=[anywhere] * 7,
        out_specs=(vmem, vmem),
        scratch_shapes=[
            pltpu.VMEM(inputs.shape, BF16),
            pltpu.VMEM(velocity.shape, BF16),
            pltpu.VMEM(gains.shape, F32),
            pltpu.VMEM(gates.shape, F32),
            pltpu.VMEM(lengths.shape, jnp.int32),
            pltpu.VMEM(steps.shape, jnp.int32),
            pltpu.VMEM((sections, nz, chunk, width), BF16),
            pltpu.VMEM((width, deep), BF16),
            pltpu.VMEM((nx, SMALL_ROWS, LANES), F32),
            pltpu.VMEM((LANES, LANES), F32),
            pltpu.VMEM((sections, deep, LANES), F32),
            pltpu.VMEM((sections, deep, LANES), F32),
            pltpu.VMEM((sections, own, LANES), F32),
            pltpu.VMEM((2, HALVES * nx, chunk, LANES), BF16),
            pltpu.VMEM((sections, nt, own, LANES), BF16),
            pltpu.VMEM((sections, nx, block, LANES), BF16),
            pltpu.VMEM((sections, nx, block, LANES), BF16),
            pltpu.VMEM((sections, own, LANES), F32),
            pltpu.VMEM((sections, own, LANES), F32),
            pltpu.VMEM((sections, own, LANES), F32),
            pltpu.VMEM((sections, 1, LANES), F32),
            pltpu.VMEM((sections, 1, LANES), F32),
            pltpu.VMEM((sections, own, LANES), F32),
            pltpu.VMEM((sections, nx, block, LANES), BF16),
            pltpu.VMEM((sections, nt, block, LANES), BF16),
            pltpu.VMEM((sections, nt, block, LANES), BF16),
            pltpu.VMEM((sections, nz, chunk, width), BF16),
            pltpu.VMEM((sections, ups, chunk, width), BF16),
            pltpu.VMEM((sections, max(downs, 1), chunk, width), BF16),
            pltpu.VMEM((sections, chunk, width), BF16),
            pltpu.VMEM((nx, chunk, width), BF16),
            pltpu.VMEM((LANES, LANES), F32),
            pltpu.VMEM((4, 8, LANES), F32),
            pltpu.VMEM((max(nz // 4, 1), 8, LANES), F32),
            pltpu.VMEM((nx, 8, LANES), F32),
            dma((sends,)),
            dma((1 + sections,)),
            dma((6,)),
            dma((nx,)),
            dma((nx,)),
            dma((sections, ups)),
            dma((sections, max(downs, 1))),
            dma((sections, nt)),
            dma((sections, nx)),
            dma((sections, nx)),
            dma((sections, nt)),
            dma((sections, ups)),
            dma((sections, max(downs, 1))),
            dma((nx,)),
            dma((4,)),
            dma((max(nz // 4, 1),)),
            dma((nx,)),
        ],
        compiler_params=pltpu.CompilerParams(
            collective_id=0, has_side_effects=True, vmem_limit_bytes=64 * 1024 * 1024
        ),
        name="sections",
    )(weights, inputs, velocity, gains, gates, lengths, steps)
    return pl.pallas_call(
        results,
        out_shape=(
            jax.ShapeDtypeStruct((1, nx * chunk, width), F32),
            jax.ShapeDtypeStruct((1, width), F32),
            jax.ShapeDtypeStruct((1, width), F32),
        ),
        in_specs=[vmem, vmem],
        out_specs=(vmem, vmem, vmem),
        name="results",
    )(parts, rows)


def solution(mesh):
    placed = (
        P(None, "dp", "tensor"),
        P(None, "dp", "tensor"),
        P("section", "dp", "tensor"),
        P("section", None),
        P("section", "tensor"),
        P("dp", None),
        P("dp", None),
    )

    def whole(*args):
        return jax.shard_map(
            local, mesh=mesh, in_specs=placed,
            out_specs=(P("section", "dp", "tensor"), P("section", "tensor"), P("section", "tensor")),
            check_vma=False,
        )(*args)

    return whole
```

```python
import functools
import math

import jax
import jax.numpy as jnp
from jax import lax
from jax.experimental import pallas as pl
from jax.experimental.pallas import tpu as pltpu
from jax.sharding import PartitionSpec as P

MESH = pl.DeviceIdType.MESH
F32 = jnp.float32
BF16 = jnp.bfloat16
NSTEPS = 50
LIVE_PER_CLIP = 100
EPS = 1e-06
LANES = 128
HALVES = 2
SMALL_ROWS = 24
TAIL = 16
PARTS_AT = 124
GATHER_RELAYS = ((0, 2, 4, 6), (0, 1, 2, 3, 4, 6), (0, 1, 2, 3, 4, 5, 6, 7), (0, 1, 2, 3, 4, 5, 6, 7))
GATHER_START = (0, 0, 1, 3)
SCATTER_REACH = (2, 2, 2, 2)
SCATTER_START = (6, 4, 2, 0)


def split3(value):
    first = value.astype(BF16)
    rest = value - first.astype(F32)
    second = rest.astype(BF16)
    third = (rest - second.astype(F32)).astype(BF16)
    return first, second, third


def stat_rows(one, two):
    rows = [r.astype(F32) for r in split3(one) + split3(two)]
    rows.append(jnp.zeros((TAIL - 6, LANES), F32))
    return jnp.concatenate(rows, axis=0).astype(BF16)


def joined(block):
    block = block.astype(F32)
    one = block[0:1] + block[1:2] + block[2:3]
    two = block[3:4] + block[4:5] + block[5:6]
    return one, two


def kernel(
    nx, nt, nz,
    w_in, inputs_in, velocity_in, gains_in, gates_in, lengths_in, steps_in,
    gw_part, row_part,
    inputs, velocity, gains, gates, lengths, steps,
    wbuf, wt, small_src, small, gainb, gtail, gateb, picked, abuf, bsend, bbuf,
    projb, gelub, slopeb, meanb, invb, ub, dbuf, qsend, qbuf, dwbuf, rs_up, rs_down,
    gw_send, gw_in, vacc, v1, v2, v3,
    send_sem, local_sem, load_sem, w_sem, small_sem, up_sem, down_sem, a_sem, b_sem, d_sem, q_sem,
    rsu_sem, rsd_sem, gw_sem, v1_sem, v2_sem, v3_sem,
):
    sections = nx
    chunk = gates.shape[1] // (HALVES * nx)
    width = gates.shape[1]
    own = HALVES * chunk
    deep = nt * own
    model = nt * width
    ups, downs = nz // 2, nz // 2 - 1
    zb = 4
    za = nz // zb
    x = lax.axis_index("section")
    t = lax.axis_index("tensor")
    z = lax.axis_index("dp")
    above = lax.rem(z + 1, nz)
    group, member = z // zb, lax.rem(z, zb)

    small[...] = jnp.zeros_like(small)
    barrier = pltpu.get_barrier_semaphore()
    greeted = 0

    def greet(axis, index):
        pl.semaphore_signal(barrier, inc=1, device_id={axis: index}, device_id_type=MESH)

    for d in range(1, nx):
        greet("section", lax.rem(x + d, nx))
        greeted += 1
    far = max(SCATTER_REACH)
    for d in range(1, far + 1):
        greet("dp", lax.rem(z + d, nz))
        greet("dp", lax.rem(z + nz - d, nz))
        greeted += 2
    for d in range(1, nt):
        greet("tensor", lax.rem(t + d, nt))
        greeted += 1

    far_x = sorted(range(1, nx), key=lambda d: -min(d, nx - d))
    far_t = sorted(range(1, nt), key=lambda d: -min(d, nt - d))
    sends = []

    def put(src, dst, recv, axis, index):
        copy = pltpu.make_async_remote_copy(
            src_ref=src, dst_ref=dst, send_sem=send_sem.at[len(sends)], recv_sem=recv,
            device_id={axis: index}, device_id_type=MESH,
        )
        copy.start()
        sends.append(copy)

    def got(dst, recv):
        pltpu.make_async_remote_copy(
            src_ref=dst, dst_ref=dst, send_sem=send_sem.at[0], recv_sem=recv,
            device_id={"dp": above}, device_id_type=MESH,
        ).wait_recv()

    loads = [
        pltpu.make_async_copy(src, dst, load_sem.at[i])
        for i, (src, dst) in enumerate((
            (gains_in, gains), (gates_in, gates), (inputs_in, inputs), (velocity_in, velocity),
            (lengths_in, lengths), (steps_in, steps),
        ))
    ]
    for load in loads:
        load.start()
    own_rows = pl.ds(pl.multiple_of(x * chunk, 16), chunk)
    keep = pltpu.make_async_copy(w_in.at[0, own_rows], wbuf.at[x, z], local_sem.at[0])
    keep.start()
    small_src[...] = jnp.zeros_like(small_src)
    for load in loads:
        load.wait()
    for to in range(nx):
        for unit in range(nz):
            at = unit * (width // HALVES) + to * chunk
            small_src[to, unit:unit + 1, 0:chunk] = gains[0:1, at:at + chunk]
        for half in range(HALVES):
            at = half * (width // HALVES) + to * chunk
            small_src[to, 16 + half:17 + half, 0:chunk] = gates[0:1, at:at + chunk]

    pl.semaphore_wait(barrier, greeted)

    for d in far_x:
        to = lax.rem(x + d, nx)
        rows = pl.ds(pl.multiple_of(to * chunk, 16), chunk)
        put(w_in.at[0, rows], wbuf.at[x, z], w_sem.at[x], "section", to)
    small_at = pl.ds(pl.multiple_of(x * SMALL_ROWS, 8), SMALL_ROWS)
    for d in range(1, nx):
        to = lax.rem(x + d, nx)
        put(small_src.at[to], small.at[small_at], small_sem.at[x], "section", to)
    small[small_at] = small_src[x]
    keep.wait()

    def wait_piece(s):
        @pl.when(x != s)
        def _():
            got(wbuf.at[s, z], w_sem.at[s])

    def stages(reach):
        return -(-ups // reach)

    def lanes_of(s, up, down):
        first, second = (ups, downs) if s % 2 == 0 else (downs, ups)
        return (1, first, up), (-1, second, down)

    def gather_event(s, j):
        relays = [r for r in GATHER_RELAYS[s] if r < ups]
        if j == 0:
            wait_piece(s)
        for way, total, sem in lanes_of(s, up_sem, down_sem):
            if j == len(relays):
                for q in range(1, total + 1):
                    if q not in relays:
                        got(wbuf.at[s, lax.rem(z - way * q + nz, nz)], sem.at[s, q - 1])
                continue
            gone = relays[j]
            last = min(total, (relays + [ups])[j + 1])
            piece = wbuf.at[s, lax.rem(z - way * gone + nz, nz)]
            if 0 < gone <= total:
                got(piece, sem.at[s, gone - 1])
            for d in range(last - gone, 0, -1):
                put(piece, piece, sem.at[s, gone + d - 1], "dp", lax.rem(z + way * d + nz, nz))

    events = sorted(
        (j + GATHER_START[s], s, j) for s in range(sections)
        for j in range(sum(r < ups for r in GATHER_RELAYS[s]) + 1)
    )

    def gather_until(key):
        while events and events[0][0] <= key:
            _, s, j = events.pop(0)
            gather_event(s, j)

    def gather_all_of(s):
        while any(event[1] == s for event in events):
            _, section, j = events.pop(0)
            gather_event(section, j)

    gather_until(0)

    lane = lax.broadcasted_iota(jnp.int32, (own, LANES), 1)

    micro, cap = inputs.shape[0], inputs.shape[1]
    slot = lax.broadcasted_iota(jnp.int32, (cap, LANES), 1)
    row = lax.broadcasted_iota(jnp.int32, (cap, LANES), 0)
    first = jnp.zeros((1, 1), jnp.int32)
    factor = jnp.zeros((own, LANES), F32)
    start_block = jnp.zeros((width, LANES), F32)
    target_block = jnp.zeros((width, LANES), F32)
    over_rows = (((0,), (0,)), ((), ()))
    for m in range(micro):
        count = lengths[0:1, m:m + 1]
        chosen = jnp.where((slot - row == first) & (row < count), 1.0, 0.0).astype(BF16)
        start_block += lax.dot_general(inputs[m], chosen, over_rows, preferred_element_type=F32)
        target_block += lax.dot_general(velocity[m], chosen, over_rows, preferred_element_type=F32)
        step = jnp.broadcast_to(steps[0:1, m:m + 1], (own, LANES)).astype(F32)
        weighting = 1.0 / (0.1 + (step + 0.5) / NSTEPS)
        inside = (lane >= first) & (lane < first + count)
        factor = jnp.where(inside, weighting / math.sqrt(LIVE_PER_CLIP * nz), factor)
        first = first + count
    picked[0] = start_block.astype(BF16).reshape(HALVES * nx, chunk, LANES)
    picked[1] = target_block.astype(BF16).reshape(HALVES * nx, chunk, LANES)

    def own_part(which):
        return jnp.concatenate([picked[which, half * nx + x] for half in range(HALVES)], axis=0)

    abuf[0, t] = own_part(0)

    def a_sends(s):
        for d in far_t:
            put(abuf.at[s, t], abuf.at[s, t], a_sem.at[s, t], "tensor", lax.rem(t + d, nt))

    a_sends(0)
    gather_until(1)

    for d in range(1, nx):
        at = lax.rem(x + d, nx)
        got(small.at[pl.ds(pl.multiple_of(at * SMALL_ROWS, 8), SMALL_ROWS)], small_sem.at[at])
    columns = jnp.transpose(small[...])
    wide_lane = lax.broadcasted_iota(jnp.int32, (chunk, LANES), 1)

    def spread_gains(s):
        for unit in range(nz):
            at = s * SMALL_ROWS + unit
            part = jnp.broadcast_to(columns[0:chunk, at:at + 1], (chunk, LANES))
            gainb[s, unit * chunk:(unit + 1) * chunk] = part
            a, b, c = (p.astype(F32) for p in split3(part))
            tail = jnp.where(wide_lane == PARTS_AT + 1, a, 0.0)
            tail = jnp.where(wide_lane == PARTS_AT + 2, b, tail)
            tail = jnp.where(wide_lane == PARTS_AT + 3, c, tail)
            gtail[s, unit * chunk:(unit + 1) * chunk] = tail
        for half in range(HALVES):
            at = s * SMALL_ROWS + 16 + half
            part = jnp.broadcast_to(columns[0:chunk, at:at + 1], (chunk, LANES))
            gateb[s, half * chunk:(half + 1) * chunk] = part

    for s in range(sections):
        spread_gains(s)
        if s < 2:
            gather_until(2 + s)

    factor = jnp.where(lane < LIVE_PER_CLIP, factor, 0.0)

    def key_after(s):
        return len(GATHER_RELAYS[0]) + 2 * s + 1

    coeff = math.sqrt(2.0 / math.pi)
    state = None
    for s in range(sections):
        if s > 0:
            abuf[s, t] = state
            a_sends(s)
        gather_all_of(s)
        weight = wbuf[s].reshape(deep, width)
        wt[...] = jnp.transpose(weight)
        for d in range(1, nt):
            at = lax.rem(t + d, nt)
            got(abuf.at[s, at], a_sem.at[s, at])
        values = abuf[s].reshape(deep, LANES).astype(F32)
        slice_mean = jnp.sum(values, axis=0, keepdims=True) * (1.0 / deep)
        centred = values - slice_mean
        slice_square = jnp.sum(centred * centred, axis=0, keepdims=True)
        operand = (centred * gainb[s] + gtail[s]).astype(BF16)
        partial = jnp.dot(wt[...], operand, preferred_element_type=F32)
        rounding = partial - partial.astype(BF16).astype(F32)
        all_lane = lax.broadcasted_iota(jnp.int32, (width, LANES), 1)
        partial = jnp.where(
            all_lane == PARTS_AT, pltpu.roll(rounding, LANES - 1, 1), partial
        ).astype(BF16)
        stats = stat_rows(slice_mean, slice_square)
        for to in range(nx):
            for half in range(HALVES):
                at = half * (width // HALVES) + to * chunk
                bsend[s, to, half * chunk:(half + 1) * chunk] = partial[at:at + chunk]
            bsend[s, to, own:own + TAIL] = stats
        for d in far_x:
            to = lax.rem(x + d, nx)
            put(bsend.at[s, to], bbuf.at[s, x], b_sem.at[s, x], "section", to)
        bbuf[s, x] = bsend[s, x]
        gather_until(key_after(s))
        for d in range(1, nx):
            at = lax.rem(x + d, nx)
            got(bbuf.at[s, at], b_sem.at[s, at])
        summed = jnp.zeros((own, LANES), F32)
        means, squares, sums = [], [], []
        for at in range(nx):
            block = bbuf[s, at, 0:own].astype(F32)
            summed += block
            sums.append(
                jnp.sum(jnp.where(lane >= PARTS_AT, block, 0.0), axis=1, keepdims=True)
            )
            one, two = joined(bbuf[s, at, own:own + TAIL])
            means.append(one)
            squares.append(two)
        mean = sum(means[1:], means[0]) * (1.0 / nx)
        square = sum(squares[1:], squares[0])
        for at in range(nx):
            square += deep * (means[at] - mean) * (means[at] - mean)
        inverse = lax.rsqrt(square * (1.0 / model) + EPS)
        total = jnp.where(lane < PARTS_AT, summed, 0.0)
        for at in range(nx):
            total += (means[at] - mean) * sums[at]
        v = total * inverse
        tanh = jnp.tanh(coeff * (v + 0.044715 * v * v * v))
        gelu = 0.5 * v * (1.0 + tanh)
        slope = 0.5 * (1.0 + tanh) + 0.5 * v * (1.0 - tanh * tanh) * coeff * (
            1.0 + 3.0 * 0.044715 * v * v
        )
        gate = gateb[s]
        projb[s] = v
        gelub[s] = gelu
        slopeb[s] = gate * slope
        meanb[s] = mean
        invb[s] = inverse
        ub[s] = jnp.broadcast_to(sum(sums[1:], sums[0]), (own, LANES))
        state = (abuf[s, t].astype(F32) + gate * gelu).astype(BF16)


    target = own_part(1).astype(F32)
    upstream = (factor * (state.astype(F32) - target)).astype(BF16).astype(F32)
    vacc[...] = jnp.zeros_like(vacc)

    def scatter_event(s, turn):
        reach = SCATTER_REACH[s]
        count = stages(reach)
        relay = count - turn
        mine = dwbuf[s, z].astype(F32) if relay == 0 else None
        ways = [
            (way, total, slots, sem)
            for way, total, (slots, sem) in lanes_of(s, (rs_up, rsu_sem), (rs_down, rsd_sem))
        ]
        for way, total, slots, sem in ways if turn > 0 else ():
            gone = relay * reach
            if gone >= total:
                continue
            children = range(gone + 1, min(gone + reach, total) + 1)
            for q in children:
                got(slots.at[s, q - 1], sem.at[s, q - 1])
            if relay > 0:
                mine = dwbuf[s, lax.rem(z + way * gone + nz, nz)].astype(F32)
            for q in children:
                mine = mine + slots[s, q - 1].astype(F32)
            if relay > 0:
                slots[s, gone] = mine.astype(BF16)
                to = lax.rem(z + way * reach + nz, nz)
                put(slots.at[s, gone], slots.at[s, gone - 1], sem.at[s, gone - 1], "dp", to)
        groups = (count, count - 1) if turn == 0 else (relay - 1,)
        for level in groups:
            for way, total, slots, sem in ways:
                for q in range(min(level * reach, total), (level - 1) * reach, -1):
                    if level >= 1 and (q % reach or q == total):
                        to = lax.rem(z + way * (q - (level - 1) * reach) + nz, nz)
                        term = dwbuf.at[s, lax.rem(z + way * q + nz, nz)]
                        put(term, slots.at[s, q - 1], sem.at[s, q - 1], "dp", to)
        if relay == 0:
            gw_send[s] = mine.astype(BF16)

            @pl.when(x != s)
            def _():
                put_to(gw_send.at[s], gw_in.at[x], gw_sem.at[x], s)

            @pl.when(x == s)
            def _():
                gw_in[x] = gw_send[s]

    def put_to(src, dst, recv, s):
        pltpu.make_async_remote_copy(
            src_ref=src, dst_ref=dst, send_sem=local_sem.at[1 + s], recv_sem=recv,
            device_id={"section": s}, device_id_type=MESH,
        ).start()

    back = sorted(
        (turn + SCATTER_START[s], s, turn)
        for s in range(sections) for turn in range(stages(SCATTER_REACH[s]) + 1)
    )

    def scatter_until(key):
        while back and back[0][0] <= key:
            _, s, turn = back.pop(0)
            scatter_event(s, turn)

    for turn, s in enumerate(reversed(range(sections))):
        vacc[0:own] = jnp.where(
            lane == 2 * s, jnp.sum(upstream * gelub[s], axis=1, keepdims=True), vacc[0:own]
        )
        dproj = (upstream * slopeb[s]).astype(BF16)
        exact = dproj.astype(F32)
        first_part = jnp.sum(exact * ub[s], axis=0, keepdims=True)
        second_part = jnp.sum(exact * projb[s], axis=0, keepdims=True)
        dbuf[s, x, 0:own] = dproj
        dbuf[s, x, own:own + TAIL] = stat_rows(first_part, second_part)
        for d in far_x:
            put(dbuf.at[s, x], dbuf.at[s, x], d_sem.at[s, x], "section", lax.rem(x + d, nx))
        if turn > 0:
            scatter_until(2 * turn - 1)
        mean, inverse = meanb[s], invb[s]
        normed = (
            (abuf[s].reshape(deep, LANES).astype(F32) - mean) * inverse * gainb[s]
        ).astype(BF16)
        for d in range(1, nx):
            at = lax.rem(x + d, nx)
            got(dbuf.at[s, at], d_sem.at[s, at])
        whole = jnp.concatenate(
            [dbuf[s, at, half * chunk:(half + 1) * chunk] for half in range(HALVES) for at in range(nx)],
            axis=0,
        )
        first_sum = jnp.zeros((1, LANES), F32)
        second_sum = jnp.zeros((1, LANES), F32)
        for at in range(nx):
            one, two = joined(dbuf[s, at, own:own + TAIL])
            first_sum += one
            second_sum += two
        def weight_term():
            term = lax.dot_general(
                normed, whole, (((1,), (1,)), ((), ())), preferred_element_type=F32
            )
            dwbuf[s] = term.astype(BF16).reshape(nz, chunk, width)

        if s == 0:
            weight_term()
            assert back.pop(0)[1:] == (0, 0)
            scatter_event(0, 0)
        product = jnp.dot(wbuf[s].reshape(deep, width), whole, preferred_element_type=F32).astype(BF16)
        stats = stat_rows(first_sum, second_sum)
        for to in range(nt):
            qsend[s, to, 0:own] = product[to * own:(to + 1) * own]
            qsend[s, to, own:own + TAIL] = stats
        for d in far_t:
            to = lax.rem(t + d, nt)
            put(qsend.at[s, to], qbuf.at[s, t], q_sem.at[s, t], "tensor", to)
        qbuf[s, t] = qsend[s, t]
        if s > 0:
            weight_term()
        scatter_until(2 * turn)
        for d in range(1, nt):
            at = lax.rem(t + d, nt)
            got(qbuf.at[s, at], q_sem.at[s, at])
        dnormed = jnp.zeros((own, LANES), F32)
        first_moment = jnp.zeros((1, LANES), F32)
        second_moment = jnp.zeros((1, LANES), F32)
        for at in range(nt):
            dnormed += qbuf[s, at, 0:own].astype(F32)
            one, two = joined(qbuf[s, at, own:own + TAIL])
            first_moment += one
            second_moment += two
        xhat = (abuf[s, t].astype(F32) - mean) * inverse
        vacc[0:own] = jnp.where(
            lane == 2 * s + 1, jnp.sum(dnormed * xhat, axis=1, keepdims=True), vacc[0:own]
        )
        if s > 0:
            gain = gainb[s, pl.ds(pl.multiple_of(t * own, 8), own)]
            change = dnormed * gain - first_moment * (1.0 / model) - xhat * (
                second_moment * (1.0 / model)
            )
            upstream = (upstream + inverse * change).astype(BF16).astype(F32)

    v1[member] = jnp.transpose(vacc[...])[0:8]
    for d in range(1, zb):
        to = group * zb + lax.rem(member + d, zb)
        put(v1.at[member], v1.at[member], v1_sem.at[member], "dp", to)
    scatter_until(SCATTER_START[0] + 1)
    for d in range(1, zb):
        at = lax.rem(member + d, zb)
        got(v1.at[at], v1_sem.at[at])
    v2[group] = v1[0] + v1[1] + v1[2] + v1[3]
    for d in range(1, za):
        to = lax.rem(group + d, za) * zb + member
        put(v2.at[group], v2.at[group], v2_sem.at[group], "dp", to)
    scatter_until(SCATTER_START[0] + stages(SCATTER_REACH[0]) - 1)
    for d in range(1, za):
        at = lax.rem(group + d, za)
        got(v2.at[at], v2_sem.at[at])
    full = v2[0]
    for at in range(1, za):
        full = full + v2[at]
    v3[x] = full
    for d in far_x:
        put(v3.at[x], v3.at[x], v3_sem.at[x], "section", lax.rem(x + d, nx))
    while back:
        _, s, turn = back.pop(0)
        scatter_event(s, turn)
    for d in range(1, nx):
        at = lax.rem(x + d, nx)
        got(v3.at[at], v3_sem.at[at])
    for at in range(nx):
        tile = v3[at]
        gate_row, gain_row = tile[0:1], tile[1:2]
        for s in range(1, sections):
            gate_row = jnp.where(x == s, tile[2 * s:2 * s + 1], gate_row)
            gain_row = jnp.where(x == s, tile[2 * s + 1:2 * s + 2], gain_row)
        for half in range(HALVES):
            to = half * (width // HALVES) + at * chunk
            row_part[0:1, to:to + chunk] = gate_row[:, half * chunk:(half + 1) * chunk]
            row_part[1:2, to:to + chunk] = gain_row[:, half * chunk:(half + 1) * chunk]
    for d in range(1, nx):
        at = lax.rem(x + d, nx)
        got(gw_in.at[at], gw_sem.at[at])
    gw_part[...] = gw_in[...]

    for copy in sends:
        copy.wait_send()
    for s in range(sections):
        @pl.when(x != s)
        def _():
            pltpu.make_async_remote_copy(
                src_ref=gw_send.at[s], dst_ref=gw_in.at[x], send_sem=local_sem.at[1 + s],
                recv_sem=gw_sem.at[x], device_id={"section": s}, device_id_type=MESH,
            ).wait_send()


def results(parts, rows, weight_out, gain_out, gate_out):
    chunk = parts.shape[1]
    for at in range(parts.shape[0]):
        weight_out[0, at * chunk:(at + 1) * chunk] = parts[at].astype(F32)
    gate_out[...] = rows[0:1]
    gain_out[...] = rows[1:2]


def local(inputs, velocity, weights, gains, gates, lengths, steps):
    nx, nt, nz = lax.axis_size("section"), lax.axis_size("tensor"), lax.axis_size("dp")
    sections = nx
    width = inputs.shape[2]
    chunk = width // (HALVES * nx)
    own = HALVES * chunk
    deep = nt * own
    ups, downs = nz // 2, nz // 2 - 1
    block = own + TAIL
    sends = (
        2 * (nx - 1) + 2 * sections * (ups + downs) + 2 * sections * (nt - 1)
        + 2 * sections * (nx - 1) + 3 + nz // 4 - 1 + nx - 1
    )
    dma = pltpu.SemaphoreType.DMA
    vmem = pl.BlockSpec(memory_space=pltpu.VMEM)
    anywhere = pl.BlockSpec(memory_space=pltpu.HBM)
    parts, rows = pl.pallas_call(
        functools.partial(kernel, nx, nt, nz),
        out_shape=(
            jax.ShapeDtypeStruct((nx, chunk, width), BF16),
            jax.ShapeDtypeStruct((2, width), F32),
        ),
        in_specs=[anywhere] * 7,
        out_specs=(vmem, vmem),
        scratch_shapes=[
            pltpu.VMEM(inputs.shape, BF16),
            pltpu.VMEM(velocity.shape, BF16),
            pltpu.VMEM(gains.shape, F32),
            pltpu.VMEM(gates.shape, F32),
            pltpu.VMEM(lengths.shape, jnp.int32),
            pltpu.VMEM(steps.shape, jnp.int32),
            pltpu.VMEM((sections, nz, chunk, width), BF16),
            pltpu.VMEM((width, deep), BF16),
            pltpu.VMEM((nx, SMALL_ROWS, LANES), F32),
            pltpu.VMEM((LANES, LANES), F32),
            pltpu.VMEM((sections, deep, LANES), F32),
            pltpu.VMEM((sections, deep, LANES), F32),
            pltpu.VMEM((sections, own, LANES), F32),
            pltpu.VMEM((2, HALVES * nx, chunk, LANES), BF16),
            pltpu.VMEM((sections, nt, own, LANES), BF16),
            pltpu.VMEM((sections, nx, block, LANES), BF16),
            pltpu.VMEM((sections, nx, block, LANES), BF16),
            pltpu.VMEM((sections, own, LANES), F32),
            pltpu.VMEM((sections, own, LANES), F32),
            pltpu.VMEM((sections, own, LANES), F32),
            pltpu.VMEM((sections, 1, LANES), F32),
            pltpu.VMEM((sections, 1, LANES), F32),
            pltpu.VMEM((sections, own, LANES), F32),
            pltpu.VMEM((sections, nx, block, LANES), BF16),
            pltpu.VMEM((sections, nt, block, LANES), BF16),
            pltpu.VMEM((sections, nt, block, LANES), BF16),
            pltpu.VMEM((sections, nz, chunk, width), BF16),
            pltpu.VMEM((sections, ups, chunk, width), BF16),
            pltpu.VMEM((sections, ups, chunk, width), BF16),
            pltpu.VMEM((sections, chunk, width), BF16),
            pltpu.VMEM((nx, chunk, width), BF16),
            pltpu.VMEM((LANES, LANES), F32),
            pltpu.VMEM((4, 8, LANES), F32),
            pltpu.VMEM((max(nz // 4, 1), 8, LANES), F32),
            pltpu.VMEM((nx, 8, LANES), F32),
            dma((sends,)),
            dma((1 + sections,)),
            dma((6,)),
            dma((nx,)),
            dma((nx,)),
            dma((sections, ups)),
            dma((sections, ups)),
            dma((sections, nt)),
            dma((sections, nx)),
            dma((sections, nx)),
            dma((sections, nt)),
            dma((sections, ups)),
            dma((sections, ups)),
            dma((nx,)),
            dma((4,)),
            dma((max(nz // 4, 1),)),
            dma((nx,)),
        ],
        compiler_params=pltpu.CompilerParams(
            collective_id=0, has_side_effects=True, vmem_limit_bytes=64 * 1024 * 1024
        ),
        name="sections",
    )(weights, inputs, velocity, gains, gates, lengths, steps)
    return pl.pallas_call(
        results,
        out_shape=(
            jax.ShapeDtypeStruct((1, nx * chunk, width), F32),
            jax.ShapeDtypeStruct((1, width), F32),
            jax.ShapeDtypeStruct((1, width), F32),
        ),
        in_specs=[vmem, vmem],
        out_specs=(vmem, vmem, vmem),
        name="results",
    )(parts, rows)


def solution(mesh):
    placed = (
        P(None, "dp", "tensor"),
        P(None, "dp", "tensor"),
        P("section", "dp", "tensor"),
        P("section", None),
        P("section", "tensor"),
        P("dp", None),
        P("dp", None),
    )

    def whole(*args):
        return jax.shard_map(
            local, mesh=mesh, in_specs=placed,
            out_specs=(P("section", "dp", "tensor"), P("section", "tensor"), P("section", "tensor")),
            check_vma=False,
        )(*args)

    return whole
```

```python
import functools
import math

import jax
import jax.numpy as jnp
from jax import lax
from jax.experimental import pallas as pl
from jax.experimental.pallas import tpu as pltpu
from jax.sharding import PartitionSpec as P

MESH = pl.DeviceIdType.MESH
F32 = jnp.float32
BF16 = jnp.bfloat16
NSTEPS = 50
LIVE_PER_CLIP = 100
EPS = 1e-06
LANES = 128
HALVES = 2
SMALL_ROWS = 24
TAIL = 16
PARTS_AT = 124
GATHER_RELAYS = ((0, 3, 6), (0, 1, 2, 3, 4, 6), (0, 1, 2, 3, 4, 5, 6, 7), (0, 1, 2, 3, 4, 5, 6, 7))
GATHER_START = (0, 0, 0, 2)
SCATTER_REACH = (2, 2, 2, 2)
SCATTER_START = (6, 4, 2, 0)


def split3(value):
    first = value.astype(BF16)
    rest = value - first.astype(F32)
    second = rest.astype(BF16)
    third = (rest - second.astype(F32)).astype(BF16)
    return first, second, third


def stat_rows(one, two):
    rows = [r.astype(F32) for r in split3(one) + split3(two)]
    rows.append(jnp.zeros((TAIL - 6, LANES), F32))
    return jnp.concatenate(rows, axis=0).astype(BF16)


def joined(block):
    block = block.astype(F32)
    one = block[0:1] + block[1:2] + block[2:3]
    two = block[3:4] + block[4:5] + block[5:6]
    return one, two


def kernel(
    nx, nt, nz,
    w_in, inputs_in, velocity_in, gains_in, gates_in, lengths_in, steps_in,
    gw_part, row_part,
    inputs, velocity, gains, gates, lengths, steps,
    wbuf, wt, small_src, small, gainb, gtail, gateb, picked, abuf, bsend, bbuf,
    projb, gelub, slopeb, meanb, invb, ub, dbuf, qsend, qbuf, dwbuf, rs_up, rs_down,
    gw_send, gw_in, vacc, v1, v2, v3,
    send_sem, local_sem, load_sem, w_sem, small_sem, up_sem, down_sem, a_sem, b_sem, d_sem, q_sem,
    rsu_sem, rsd_sem, gw_sem, v1_sem, v2_sem, v3_sem,
):
    sections = nx
    chunk = gates.shape[1] // (HALVES * nx)
    width = gates.shape[1]
    own = HALVES * chunk
    deep = nt * own
    model = nt * width
    ups, downs = nz // 2, nz // 2 - 1
    zb = 4
    za = nz // zb
    x = lax.axis_index("section")
    t = lax.axis_index("tensor")
    z = lax.axis_index("dp")
    above = lax.rem(z + 1, nz)
    group, member = z // zb, lax.rem(z, zb)

    small[...] = jnp.zeros_like(small)
    barrier = pltpu.get_barrier_semaphore()
    greeted = 0

    def greet(axis, index):
        pl.semaphore_signal(barrier, inc=1, device_id={axis: index}, device_id_type=MESH)

    for d in range(1, nx):
        greet("section", lax.rem(x + d, nx))
        greeted += 1
    far = 3
    for d in range(1, far + 1):
        greet("dp", lax.rem(z + d, nz))
        greet("dp", lax.rem(z + nz - d, nz))
        greeted += 2
    for d in range(1, nt):
        greet("tensor", lax.rem(t + d, nt))
        greeted += 1

    far_x = sorted(range(1, nx), key=lambda d: -min(d, nx - d))
    far_t = sorted(range(1, nt), key=lambda d: -min(d, nt - d))
    sends = []

    def put(src, dst, recv, axis, index):
        copy = pltpu.make_async_remote_copy(
            src_ref=src, dst_ref=dst, send_sem=send_sem.at[len(sends)], recv_sem=recv,
            device_id={axis: index}, device_id_type=MESH,
        )
        copy.start()
        sends.append(copy)

    finished = []

    def finish_sends(count):
        while len(finished) < count:
            copy = sends[len(finished)]
            copy.wait_send()
            finished.append(copy)

    def got(dst, recv):
        pltpu.make_async_remote_copy(
            src_ref=dst, dst_ref=dst, send_sem=send_sem.at[0], recv_sem=recv,
            device_id={"dp": above}, device_id_type=MESH,
        ).wait_recv()

    loads = [
        pltpu.make_async_copy(src, dst, load_sem.at[i])
        for i, (src, dst) in enumerate((
            (gains_in, gains), (gates_in, gates), (inputs_in, inputs), (velocity_in, velocity),
            (lengths_in, lengths), (steps_in, steps),
        ))
    ]
    for load in loads:
        load.start()
    own_rows = pl.ds(pl.multiple_of(x * chunk, 16), chunk)
    keep = pltpu.make_async_copy(w_in.at[0, own_rows], wbuf.at[x, z], local_sem.at[0])
    keep.start()
    small_src[...] = jnp.zeros_like(small_src)
    for load in loads:
        load.wait()
    for to in range(nx):
        for unit in range(nz):
            at = unit * (width // HALVES) + to * chunk
            small_src[to, unit:unit + 1, 0:chunk] = gains[0:1, at:at + chunk]
        for half in range(HALVES):
            at = half * (width // HALVES) + to * chunk
            small_src[to, 16 + half:17 + half, 0:chunk] = gates[0:1, at:at + chunk]

    pl.semaphore_wait(barrier, greeted)

    for d in far_x:
        to = lax.rem(x + d, nx)
        rows = pl.ds(pl.multiple_of(to * chunk, 16), chunk)
        put(w_in.at[0, rows], wbuf.at[x, z], w_sem.at[x], "section", to)
    small_at = pl.ds(pl.multiple_of(x * SMALL_ROWS, 8), SMALL_ROWS)
    for d in range(1, nx):
        to = lax.rem(x + d, nx)
        put(small_src.at[to], small.at[small_at], small_sem.at[x], "section", to)
    small[small_at] = small_src[x]
    keep.wait()

    def wait_piece(s):
        @pl.when(x != s)
        def _():
            got(wbuf.at[s, z], w_sem.at[s])

    def stages(reach):
        return -(-ups // reach)

    def lanes_of(s, up, down):
        first, second = (ups, downs) if s % 2 == 0 else (downs, ups)
        return (1, first, up), (-1, second, down)

    def gather_event(s, j):
        relays = [r for r in GATHER_RELAYS[s] if r < ups]
        if j == 0:
            wait_piece(s)
        for way, total, sem in lanes_of(s, up_sem, down_sem):
            if j == len(relays):
                for q in range(1, total + 1):
                    if q not in relays:
                        got(wbuf.at[s, lax.rem(z - way * q + nz, nz)], sem.at[s, q - 1])
                continue
            gone = relays[j]
            last = min(total, (relays + [ups])[j + 1])
            piece = wbuf.at[s, lax.rem(z - way * gone + nz, nz)]
            if 0 < gone <= total:
                got(piece, sem.at[s, gone - 1])
            for d in range(last - gone, 0, -1):
                put(piece, piece, sem.at[s, gone + d - 1], "dp", lax.rem(z + way * d + nz, nz))

    events = sorted(
        (j + GATHER_START[s], s, j) for s in range(sections)
        for j in range(sum(r < ups for r in GATHER_RELAYS[s]) + 1)
    )

    def gather_until(key):
        while events and events[0][0] <= key:
            _, s, j = events.pop(0)
            gather_event(s, j)

    def gather_all_of(s):
        while any(event[1] == s for event in events):
            _, section, j = events.pop(0)
            gather_event(section, j)

    gather_until(0)

    lane = lax.broadcasted_iota(jnp.int32, (own, LANES), 1)

    micro, cap = inputs.shape[0], inputs.shape[1]
    slot = lax.broadcasted_iota(jnp.int32, (cap, LANES), 1)
    row = lax.broadcasted_iota(jnp.int32, (cap, LANES), 0)
    first = jnp.zeros((1, 1), jnp.int32)
    factor = jnp.zeros((own, LANES), F32)
    start_block = jnp.zeros((width, LANES), F32)
    target_block = jnp.zeros((width, LANES), F32)
    over_rows = (((0,), (0,)), ((), ()))
    for m in range(micro):
        count = lengths[0:1, m:m + 1]
        chosen = jnp.where((slot - row == first) & (row < count), 1.0, 0.0).astype(BF16)
        start_block += lax.dot_general(inputs[m], chosen, over_rows, preferred_element_type=F32)
        target_block += lax.dot_general(velocity[m], chosen, over_rows, preferred_element_type=F32)
        step = jnp.broadcast_to(steps[0:1, m:m + 1], (own, LANES)).astype(F32)
        weighting = 1.0 / (0.1 + (step + 0.5) / NSTEPS)
        inside = (lane >= first) & (lane < first + count)
        factor = jnp.where(inside, weighting / math.sqrt(LIVE_PER_CLIP * nz), factor)
        first = first + count
    picked[0] = start_block.astype(BF16).reshape(HALVES * nx, chunk, LANES)
    picked[1] = target_block.astype(BF16).reshape(HALVES * nx, chunk, LANES)

    def own_part(which):
        return jnp.concatenate([picked[which, half * nx + x] for half in range(HALVES)], axis=0)

    abuf[0, t] = own_part(0)

    def a_sends(s):
        for d in far_t:
            put(abuf.at[s, t], abuf.at[s, t], a_sem.at[s, t], "tensor", lax.rem(t + d, nt))

    a_sends(0)
    gather_until(1)

    for d in range(1, nx):
        at = lax.rem(x + d, nx)
        got(small.at[pl.ds(pl.multiple_of(at * SMALL_ROWS, 8), SMALL_ROWS)], small_sem.at[at])
    columns = jnp.transpose(small[...])
    wide_lane = lax.broadcasted_iota(jnp.int32, (chunk, LANES), 1)

    def spread_gains(s):
        for unit in range(nz):
            at = s * SMALL_ROWS + unit
            part = jnp.broadcast_to(columns[0:chunk, at:at + 1], (chunk, LANES))
            gainb[s, unit * chunk:(unit + 1) * chunk] = part
            a, b, c = (p.astype(F32) for p in split3(part))
            tail = jnp.where(wide_lane == PARTS_AT + 1, a, 0.0)
            tail = jnp.where(wide_lane == PARTS_AT + 2, b, tail)
            tail = jnp.where(wide_lane == PARTS_AT + 3, c, tail)
            gtail[s, unit * chunk:(unit + 1) * chunk] = tail
        for half in range(HALVES):
            at = s * SMALL_ROWS + 16 + half
            part = jnp.broadcast_to(columns[0:chunk, at:at + 1], (chunk, LANES))
            gateb[s, half * chunk:(half + 1) * chunk] = part

    for s in range(sections):
        spread_gains(s)
        if s < 2:
            gather_until(2 + s)

    factor = jnp.where(lane < LIVE_PER_CLIP, factor, 0.0)

    def key_after(s):
        return len(GATHER_RELAYS[0]) + 2 * s + 1

    coeff = math.sqrt(2.0 / math.pi)
    state = None
    for s in range(sections):
        if s > 0:
            abuf[s, t] = state
            a_sends(s)
        gather_all_of(s)
        weight = wbuf[s].reshape(deep, width)
        wt[...] = jnp.transpose(weight)
        for d in range(1, nt):
            at = lax.rem(t + d, nt)
            got(abuf.at[s, at], a_sem.at[s, at])
        values = abuf[s].reshape(deep, LANES).astype(F32)
        slice_mean = jnp.sum(values, axis=0, keepdims=True) * (1.0 / deep)
        centred = values - slice_mean
        slice_square = jnp.sum(centred * centred, axis=0, keepdims=True)
        operand = (centred * gainb[s] + gtail[s]).astype(BF16)
        partial = jnp.dot(wt[...], operand, preferred_element_type=F32)
        rounding = partial - partial.astype(BF16).astype(F32)
        all_lane = lax.broadcasted_iota(jnp.int32, (width, LANES), 1)
        partial = jnp.where(
            all_lane == PARTS_AT, pltpu.roll(rounding, LANES - 1, 1), partial
        ).astype(BF16)
        stats = stat_rows(slice_mean, slice_square)
        for to in range(nx):
            for half in range(HALVES):
                at = half * (width // HALVES) + to * chunk
                bsend[s, to, half * chunk:(half + 1) * chunk] = partial[at:at + chunk]
            bsend[s, to, own:own + TAIL] = stats
        for d in far_x:
            to = lax.rem(x + d, nx)
            put(bsend.at[s, to], bbuf.at[s, x], b_sem.at[s, x], "section", to)
        bbuf[s, x] = bsend[s, x]
        gather_until(key_after(s))
        for d in range(1, nx):
            at = lax.rem(x + d, nx)
            got(bbuf.at[s, at], b_sem.at[s, at])
        summed = jnp.zeros((own, LANES), F32)
        means, squares, sums = [], [], []
        for at in range(nx):
            block = bbuf[s, at, 0:own].astype(F32)
            summed += block
            sums.append(
                jnp.sum(jnp.where(lane >= PARTS_AT, block, 0.0), axis=1, keepdims=True)
            )
            one, two = joined(bbuf[s, at, own:own + TAIL])
            means.append(one)
            squares.append(two)
        mean = sum(means[1:], means[0]) * (1.0 / nx)
        square = sum(squares[1:], squares[0])
        for at in range(nx):
            square += deep * (means[at] - mean) * (means[at] - mean)
        inverse = lax.rsqrt(square * (1.0 / model) + EPS)
        total = jnp.where(lane < PARTS_AT, summed, 0.0)
        for at in range(nx):
            total += (means[at] - mean) * sums[at]
        v = total * inverse
        tanh = jnp.tanh(coeff * (v + 0.044715 * v * v * v))
        gelu = 0.5 * v * (1.0 + tanh)
        slope = 0.5 * (1.0 + tanh) + 0.5 * v * (1.0 - tanh * tanh) * coeff * (
            1.0 + 3.0 * 0.044715 * v * v
        )
        gate = gateb[s]
        projb[s] = v
        gelub[s] = gelu
        slopeb[s] = gate * slope
        meanb[s] = mean
        invb[s] = inverse
        ub[s] = jnp.broadcast_to(sum(sums[1:], sums[0]), (own, LANES))
        state = (abuf[s, t].astype(F32) + gate * gelu).astype(BF16)


    target = own_part(1).astype(F32)
    upstream = (factor * (state.astype(F32) - target)).astype(BF16).astype(F32)
    vacc[...] = jnp.zeros_like(vacc)

    def scatter_event(s, turn):
        reach = SCATTER_REACH[s]
        count = stages(reach)
        relay = count - turn
        mine = dwbuf[s, z].astype(F32) if relay == 0 else None
        ways = [
            (way, total, slots, sem)
            for way, total, (slots, sem) in lanes_of(s, (rs_up, rsu_sem), (rs_down, rsd_sem))
        ]
        for way, total, slots, sem in ways if turn > 0 else ():
            gone = relay * reach
            if gone >= total:
                continue
            children = range(gone + 1, min(gone + reach, total) + 1)
            for q in children:
                got(slots.at[s, q - 1], sem.at[s, q - 1])
            if relay > 0:
                mine = dwbuf[s, lax.rem(z + way * gone + nz, nz)].astype(F32)
            for q in children:
                mine = mine + slots[s, q - 1].astype(F32)
            if relay > 0:
                slots[s, gone] = mine.astype(BF16)
                to = lax.rem(z + way * reach + nz, nz)
                put(slots.at[s, gone], slots.at[s, gone - 1], sem.at[s, gone - 1], "dp", to)
        groups = (count, count - 1) if turn == 0 else (relay - 1,)
        for level in groups:
            for way, total, slots, sem in ways:
                for q in range(min(level * reach, total), (level - 1) * reach, -1):
                    if level >= 1 and (q % reach or q == total):
                        to = lax.rem(z + way * (q - (level - 1) * reach) + nz, nz)
                        term = dwbuf.at[s, lax.rem(z + way * q + nz, nz)]
                        put(term, slots.at[s, q - 1], sem.at[s, q - 1], "dp", to)
        if relay == 0:
            gw_send[s] = mine.astype(BF16)

            @pl.when(x != s)
            def _():
                put_to(gw_send.at[s], gw_in.at[x], gw_sem.at[x], s)

            @pl.when(x == s)
            def _():
                gw_in[x] = gw_send[s]

    def put_to(src, dst, recv, s):
        pltpu.make_async_remote_copy(
            src_ref=src, dst_ref=dst, send_sem=local_sem.at[1 + s], recv_sem=recv,
            device_id={"section": s}, device_id_type=MESH,
        ).start()

    back = sorted(
        (turn + SCATTER_START[s], s, turn)
        for s in range(sections) for turn in range(stages(SCATTER_REACH[s]) + 1)
    )

    def scatter_until(key):
        while back and back[0][0] <= key:
            _, s, turn = back.pop(0)
            scatter_event(s, turn)

    for turn, s in enumerate(reversed(range(sections))):
        vacc[0:own] = jnp.where(
            lane == 2 * s, jnp.sum(upstream * gelub[s], axis=1, keepdims=True), vacc[0:own]
        )
        older = len(sends)
        dproj = (upstream * slopeb[s]).astype(BF16)
        exact = dproj.astype(F32)
        first_part = jnp.sum(exact * ub[s], axis=0, keepdims=True)
        second_part = jnp.sum(exact * projb[s], axis=0, keepdims=True)
        dbuf[s, x, 0:own] = dproj
        dbuf[s, x, own:own + TAIL] = stat_rows(first_part, second_part)
        for d in far_x:
            put(dbuf.at[s, x], dbuf.at[s, x], d_sem.at[s, x], "section", lax.rem(x + d, nx))
        if turn > 0:
            scatter_until(2 * turn - 1)
        mean, inverse = meanb[s], invb[s]
        normed = (
            (abuf[s].reshape(deep, LANES).astype(F32) - mean) * inverse * gainb[s]
        ).astype(BF16)
        for d in range(1, nx):
            at = lax.rem(x + d, nx)
            got(dbuf.at[s, at], d_sem.at[s, at])
        whole = jnp.concatenate(
            [dbuf[s, at, half * chunk:(half + 1) * chunk] for half in range(HALVES) for at in range(nx)],
            axis=0,
        )
        first_sum = jnp.zeros((1, LANES), F32)
        second_sum = jnp.zeros((1, LANES), F32)
        for at in range(nx):
            one, two = joined(dbuf[s, at, own:own + TAIL])
            first_sum += one
            second_sum += two
        def weight_term():
            term = lax.dot_general(
                normed, whole, (((1,), (1,)), ((), ())), preferred_element_type=F32
            )
            dwbuf[s] = term.astype(BF16).reshape(nz, chunk, width)

        if s == 0:
            weight_term()
            assert back.pop(0)[1:] == (0, 0)
            scatter_event(0, 0)
        product = jnp.dot(wbuf[s].reshape(deep, width), whole, preferred_element_type=F32).astype(BF16)
        stats = stat_rows(first_sum, second_sum)
        for to in range(nt):
            qsend[s, to, 0:own] = product[to * own:(to + 1) * own]
            qsend[s, to, own:own + TAIL] = stats
        for d in far_t:
            to = lax.rem(t + d, nt)
            put(qsend.at[s, to], qbuf.at[s, t], q_sem.at[s, t], "tensor", to)
        qbuf[s, t] = qsend[s, t]
        if s > 0:
            weight_term()
        scatter_until(2 * turn)
        finish_sends(older)
        for d in range(1, nt):
            at = lax.rem(t + d, nt)
            got(qbuf.at[s, at], q_sem.at[s, at])
        dnormed = jnp.zeros((own, LANES), F32)
        first_moment = jnp.zeros((1, LANES), F32)
        second_moment = jnp.zeros((1, LANES), F32)
        for at in range(nt):
            dnormed += qbuf[s, at, 0:own].astype(F32)
            one, two = joined(qbuf[s, at, own:own + TAIL])
            first_moment += one
            second_moment += two
        xhat = (abuf[s, t].astype(F32) - mean) * inverse
        vacc[0:own] = jnp.where(
            lane == 2 * s + 1, jnp.sum(dnormed * xhat, axis=1, keepdims=True), vacc[0:own]
        )
        if s > 0:
            gain = gainb[s, pl.ds(pl.multiple_of(t * own, 8), own)]
            change = dnormed * gain - first_moment * (1.0 / model) - xhat * (
                second_moment * (1.0 / model)
            )
            upstream = (upstream + inverse * change).astype(BF16).astype(F32)

    v1[member] = jnp.transpose(vacc[...])[0:8]
    for d in range(1, zb):
        to = group * zb + lax.rem(member + d, zb)
        put(v1.at[member], v1.at[member], v1_sem.at[member], "dp", to)
    scatter_until(SCATTER_START[0] + 1)
    finish_sends(len(sends) - 20)
    for d in range(1, zb):
        at = lax.rem(member + d, zb)
        got(v1.at[at], v1_sem.at[at])
    v2[group] = v1[0] + v1[1] + v1[2] + v1[3]
    for d in range(1, za):
        to = lax.rem(group + d, za) * zb + member
        put(v2.at[group], v2.at[group], v2_sem.at[group], "dp", to)
    scatter_until(SCATTER_START[0] + stages(SCATTER_REACH[0]) - 1)
    for d in range(1, za):
        at = lax.rem(group + d, za)
        got(v2.at[at], v2_sem.at[at])
    full = v2[0]
    for at in range(1, za):
        full = full + v2[at]
    v3[x] = full
    finish_sends(len(sends) - 6)
    for d in far_x:
        put(v3.at[x], v3.at[x], v3_sem.at[x], "section", lax.rem(x + d, nx))
    while back:
        _, s, turn = back.pop(0)
        scatter_event(s, turn)
    for d in range(1, nx):
        at = lax.rem(x + d, nx)
        got(v3.at[at], v3_sem.at[at])
    for at in range(nx):
        tile = v3[at]
        gate_row, gain_row = tile[0:1], tile[1:2]
        for s in range(1, sections):
            gate_row = jnp.where(x == s, tile[2 * s:2 * s + 1], gate_row)
            gain_row = jnp.where(x == s, tile[2 * s + 1:2 * s + 2], gain_row)
        for half in range(HALVES):
            to = half * (width // HALVES) + at * chunk
            row_part[0:1, to:to + chunk] = gate_row[:, half * chunk:(half + 1) * chunk]
            row_part[1:2, to:to + chunk] = gain_row[:, half * chunk:(half + 1) * chunk]
    for d in range(1, nx):
        at = lax.rem(x + d, nx)
        got(gw_in.at[at], gw_sem.at[at])
    gw_part[...] = gw_in[...]

    finish_sends(len(sends))
    for s in range(sections):
        @pl.when(x != s)
        def _():
            pltpu.make_async_remote_copy(
                src_ref=gw_send.at[s], dst_ref=gw_in.at[x], send_sem=local_sem.at[1 + s],
                recv_sem=gw_sem.at[x], device_id={"section": s}, device_id_type=MESH,
            ).wait_send()


def results(parts, rows, weight_out, gain_out, gate_out):
    chunk = parts.shape[1]
    for at in range(parts.shape[0]):
        weight_out[0, at * chunk:(at + 1) * chunk] = parts[at].astype(F32)
    gate_out[...] = rows[0:1]
    gain_out[...] = rows[1:2]


def local(inputs, velocity, weights, gains, gates, lengths, steps):
    nx, nt, nz = lax.axis_size("section"), lax.axis_size("tensor"), lax.axis_size("dp")
    sections = nx
    width = inputs.shape[2]
    chunk = width // (HALVES * nx)
    own = HALVES * chunk
    deep = nt * own
    ups, downs = nz // 2, nz // 2 - 1
    block = own + TAIL
    sends = (
        2 * (nx - 1) + 2 * sections * (ups + downs) + 2 * sections * (nt - 1)
        + 2 * sections * (nx - 1) + 3 + nz // 4 - 1 + nx - 1
    )
    dma = pltpu.SemaphoreType.DMA
    vmem = pl.BlockSpec(memory_space=pltpu.VMEM)
    anywhere = pl.BlockSpec(memory_space=pltpu.HBM)
    parts, rows = pl.pallas_call(
        functools.partial(kernel, nx, nt, nz),
        out_shape=(
            jax.ShapeDtypeStruct((nx, chunk, width), BF16),
            jax.ShapeDtypeStruct((2, width), F32),
        ),
        in_specs=[anywhere] * 7,
        out_specs=(vmem, vmem),
        scratch_shapes=[
            pltpu.VMEM(inputs.shape, BF16),
            pltpu.VMEM(velocity.shape, BF16),
            pltpu.VMEM(gains.shape, F32),
            pltpu.VMEM(gates.shape, F32),
            pltpu.VMEM(lengths.shape, jnp.int32),
            pltpu.VMEM(steps.shape, jnp.int32),
            pltpu.VMEM((sections, nz, chunk, width), BF16),
            pltpu.VMEM((width, deep), BF16),
            pltpu.VMEM((nx, SMALL_ROWS, LANES), F32),
            pltpu.VMEM((LANES, LANES), F32),
            pltpu.VMEM((sections, deep, LANES), F32),
            pltpu.VMEM((sections, deep, LANES), F32),
            pltpu.VMEM((sections, own, LANES), F32),
            pltpu.VMEM((2, HALVES * nx, chunk, LANES), BF16),
            pltpu.VMEM((sections, nt, own, LANES), BF16),
            pltpu.VMEM((sections, nx, block, LANES), BF16),
            pltpu.VMEM((sections, nx, block, LANES), BF16),
            pltpu.VMEM((sections, own, LANES), F32),
            pltpu.VMEM((sections, own, LANES), F32),
            pltpu.VMEM((sections, own, LANES), F32),
            pltpu.VMEM((sections, 1, LANES), F32),
            pltpu.VMEM((sections, 1, LANES), F32),
            pltpu.VMEM((sections, own, LANES), F32),
            pltpu.VMEM((sections, nx, block, LANES), BF16),
            pltpu.VMEM((sections, nt, block, LANES), BF16),
            pltpu.VMEM((sections, nt, block, LANES), BF16),
            pltpu.VMEM((sections, nz, chunk, width), BF16),
            pltpu.VMEM((sections, ups, chunk, width), BF16),
            pltpu.VMEM((sections, ups, chunk, width), BF16),
            pltpu.VMEM((sections, chunk, width), BF16),
            pltpu.VMEM((nx, chunk, width), BF16),
            pltpu.VMEM((LANES, LANES), F32),
            pltpu.VMEM((4, 8, LANES), F32),
            pltpu.VMEM((max(nz // 4, 1), 8, LANES), F32),
            pltpu.VMEM((nx, 8, LANES), F32),
            dma((sends,)),
            dma((1 + sections,)),
            dma((6,)),
            dma((nx,)),
            dma((nx,)),
            dma((sections, ups)),
            dma((sections, ups)),
            dma((sections, nt)),
            dma((sections, nx)),
            dma((sections, nx)),
            dma((sections, nt)),
            dma((sections, ups)),
            dma((sections, ups)),
            dma((nx,)),
            dma((4,)),
            dma((max(nz // 4, 1),)),
            dma((nx,)),
        ],
        compiler_params=pltpu.CompilerParams(
            collective_id=0, has_side_effects=True, vmem_limit_bytes=64 * 1024 * 1024
        ),
        name="sections",
    )(weights, inputs, velocity, gains, gates, lengths, steps)
    return pl.pallas_call(
        results,
        out_shape=(
            jax.ShapeDtypeStruct((1, nx * chunk, width), F32),
            jax.ShapeDtypeStruct((1, width), F32),
            jax.ShapeDtypeStruct((1, width), F32),
        ),
        in_specs=[vmem, vmem],
        out_specs=(vmem, vmem, vmem),
        name="results",
    )(parts, rows)


def solution(mesh):
    placed = (
        P(None, "dp", "tensor"),
        P(None, "dp", "tensor"),
        P("section", "dp", "tensor"),
        P("section", None),
        P("section", "tensor"),
        P("dp", None),
        P("dp", None),
    )

    def whole(*args):
        return jax.shard_map(
            local, mesh=mesh, in_specs=placed,
            out_specs=(P("section", "dp", "tensor"), P("section", "tensor"), P("section", "tensor")),
            check_vma=False,
        )(*args)

    return whole
```

```python
import functools
import math

import jax
import jax.numpy as jnp
from jax import lax
from jax.experimental import pallas as pl
from jax.experimental.pallas import tpu as pltpu
from jax.sharding import PartitionSpec as P

MESH = pl.DeviceIdType.MESH
F32 = jnp.float32
BF16 = jnp.bfloat16
NSTEPS = 50
LIVE_PER_CLIP = 100
EPS = 1e-06
LANES = 128
HALVES = 2
SMALL_ROWS = 24
TAIL = 16
PARTS_AT = 124
GATHER_RELAYS = ((0, 3, 6), (0, 1, 2, 3, 4, 6), (0, 1, 2, 3, 4, 5, 6, 7), (0, 1, 2, 3, 4, 5, 6, 7))
GATHER_START = (0, 0, 0, 2)
SCATTER_REACH = (2, 2, 2, 2)
SCATTER_START = (6, 4, 2, 0)


def split3(value):
    first = value.astype(BF16)
    rest = value - first.astype(F32)
    second = rest.astype(BF16)
    third = (rest - second.astype(F32)).astype(BF16)
    return first, second, third


def stat_rows(one, two):
    rows = [r.astype(F32) for r in split3(one) + split3(two)]
    rows.append(jnp.zeros((TAIL - 6, LANES), F32))
    return jnp.concatenate(rows, axis=0).astype(BF16)


def joined(block):
    block = block.astype(F32)
    one = block[0:1] + block[1:2] + block[2:3]
    two = block[3:4] + block[4:5] + block[5:6]
    return one, two


def kernel(
    nx, nt, nz,
    w_in, inputs_in, velocity_in, gains_in, gates_in, lengths_in, steps_in,
    gw_part, row_part,
    inputs, velocity, gains, gates, lengths, steps,
    wbuf, wt, small_src, small, gainb, gtail, gateb, picked, abuf, bsend, bbuf,
    projb, gelub, slopeb, meanb, invb, ub, dbuf, qsend, qbuf, dwbuf, rs_up, rs_down,
    gw_send, gw_in, vacc, v1, v2, v3,
    send_sem, local_sem, load_sem, w_sem, small_sem, up_sem, down_sem, a_sem, b_sem, d_sem, q_sem,
    rsu_sem, rsd_sem, gw_sem, v1_sem, v2_sem, v3_sem,
):
    sections = nx
    chunk = gates.shape[1] // (HALVES * nx)
    width = gates.shape[1]
    own = HALVES * chunk
    deep = nt * own
    model = nt * width
    ups, downs = nz // 2, nz // 2 - 1
    zb = 4
    za = nz // zb
    x = lax.axis_index("section")
    t = lax.axis_index("tensor")
    z = lax.axis_index("dp")
    above = lax.rem(z + 1, nz)
    group, member = z // zb, lax.rem(z, zb)

    small[...] = jnp.zeros_like(small)
    barrier = pltpu.get_barrier_semaphore()
    greeted = 0

    def greet(axis, index):
        pl.semaphore_signal(barrier, inc=1, device_id={axis: index}, device_id_type=MESH)

    for d in range(1, nx):
        greet("section", lax.rem(x + d, nx))
        greeted += 1
    far = 3
    for d in range(1, far + 1):
        greet("dp", lax.rem(z + d, nz))
        greet("dp", lax.rem(z + nz - d, nz))
        greeted += 2
    for d in range(1, nt):
        greet("tensor", lax.rem(t + d, nt))
        greeted += 1

    far_x = sorted(range(1, nx), key=lambda d: -min(d, nx - d))
    far_t = sorted(range(1, nt), key=lambda d: -min(d, nt - d))
    sends = []

    def put(src, dst, recv, axis, index):
        copy = pltpu.make_async_remote_copy(
            src_ref=src, dst_ref=dst, send_sem=send_sem.at[len(sends)], recv_sem=recv,
            device_id={axis: index}, device_id_type=MESH,
        )
        copy.start()
        sends.append(copy)

    finished = []

    def finish_sends(count):
        while len(finished) < count:
            copy = sends[len(finished)]
            copy.wait_send()
            finished.append(copy)

    def got(dst, recv):
        pltpu.make_async_remote_copy(
            src_ref=dst, dst_ref=dst, send_sem=send_sem.at[0], recv_sem=recv,
            device_id={"dp": above}, device_id_type=MESH,
        ).wait_recv()

    loads = [
        pltpu.make_async_copy(src, dst, load_sem.at[i])
        for i, (src, dst) in enumerate((
            (gains_in, gains), (gates_in, gates), (inputs_in, inputs), (velocity_in, velocity),
            (lengths_in, lengths), (steps_in, steps),
        ))
    ]
    for load in loads:
        load.start()
    own_rows = pl.ds(pl.multiple_of(x * chunk, 16), chunk)
    keep = pltpu.make_async_copy(w_in.at[0, own_rows], wbuf.at[x, z], local_sem.at[0])
    keep.start()
    small_src[...] = jnp.zeros_like(small_src)
    for load in loads:
        load.wait()
    for to in range(nx):
        for unit in range(nz):
            at = unit * (width // HALVES) + to * chunk
            small_src[to, unit:unit + 1, 0:chunk] = gains[0:1, at:at + chunk]
        for half in range(HALVES):
            at = half * (width // HALVES) + to * chunk
            small_src[to, 16 + half:17 + half, 0:chunk] = gates[0:1, at:at + chunk]

    pl.semaphore_wait(barrier, greeted)

    for d in far_x:
        to = lax.rem(x + d, nx)
        rows = pl.ds(pl.multiple_of(to * chunk, 16), chunk)
        put(w_in.at[0, rows], wbuf.at[x, z], w_sem.at[x], "section", to)
    small_at = pl.ds(pl.multiple_of(x * SMALL_ROWS, 8), SMALL_ROWS)
    for d in range(1, nx):
        to = lax.rem(x + d, nx)
        put(small_src.at[to], small.at[small_at], small_sem.at[x], "section", to)
    small[small_at] = small_src[x]
    keep.wait()

    def wait_piece(s):
        @pl.when(x != s)
        def _():
            got(wbuf.at[s, z], w_sem.at[s])

    def stages(reach):
        return -(-ups // reach)

    def lanes_of(s, up, down):
        first, second = (ups, downs) if s % 2 == 0 else (downs, ups)
        return (1, first, up), (-1, second, down)

    def gather_event(s, j):
        relays = [r for r in GATHER_RELAYS[s] if r < ups]
        if j == 0:
            wait_piece(s)
        for way, total, sem in lanes_of(s, up_sem, down_sem):
            if j == len(relays):
                for q in range(1, total + 1):
                    if q not in relays:
                        got(wbuf.at[s, lax.rem(z - way * q + nz, nz)], sem.at[s, q - 1])
                continue
            gone = relays[j]
            last = min(total, (relays + [ups])[j + 1])
            piece = wbuf.at[s, lax.rem(z - way * gone + nz, nz)]
            if 0 < gone <= total:
                got(piece, sem.at[s, gone - 1])
            for d in range(last - gone, 0, -1):
                put(piece, piece, sem.at[s, gone + d - 1], "dp", lax.rem(z + way * d + nz, nz))

    events = sorted(
        (j + GATHER_START[s], s, j) for s in range(sections)
        for j in range(sum(r < ups for r in GATHER_RELAYS[s]) + 1)
    )

    def gather_until(key):
        while events and events[0][0] <= key:
            _, s, j = events.pop(0)
            gather_event(s, j)

    def gather_all_of(s):
        while any(event[1] == s for event in events):
            _, section, j = events.pop(0)
            gather_event(section, j)

    gather_until(0)

    lane = lax.broadcasted_iota(jnp.int32, (own, LANES), 1)

    micro, cap = inputs.shape[0], inputs.shape[1]
    slot = lax.broadcasted_iota(jnp.int32, (cap, LANES), 1)
    row = lax.broadcasted_iota(jnp.int32, (cap, LANES), 0)
    first = jnp.zeros((1, 1), jnp.int32)
    factor = jnp.zeros((own, LANES), F32)
    start_block = jnp.zeros((width, LANES), F32)
    target_block = jnp.zeros((width, LANES), F32)
    over_rows = (((0,), (0,)), ((), ()))
    for m in range(micro):
        count = lengths[0:1, m:m + 1]
        chosen = jnp.where((slot - row == first) & (row < count), 1.0, 0.0).astype(BF16)
        start_block += lax.dot_general(inputs[m], chosen, over_rows, preferred_element_type=F32)
        target_block += lax.dot_general(velocity[m], chosen, over_rows, preferred_element_type=F32)
        step = jnp.broadcast_to(steps[0:1, m:m + 1], (own, LANES)).astype(F32)
        weighting = 1.0 / (0.1 + (step + 0.5) / NSTEPS)
        inside = (lane >= first) & (lane < first + count)
        factor = jnp.where(inside, weighting / math.sqrt(LIVE_PER_CLIP * nz), factor)
        first = first + count
    picked[0] = start_block.astype(BF16).reshape(HALVES * nx, chunk, LANES)
    picked[1] = target_block.astype(BF16).reshape(HALVES * nx, chunk, LANES)

    def own_part(which):
        return jnp.concatenate([picked[which, half * nx + x] for half in range(HALVES)], axis=0)

    abuf[0, t] = own_part(0)

    def a_sends(s):
        for d in far_t:
            put(abuf.at[s, t], abuf.at[s, t], a_sem.at[s, t], "tensor", lax.rem(t + d, nt))

    a_sends(0)
    gather_until(1)

    for d in range(1, nx):
        at = lax.rem(x + d, nx)
        got(small.at[pl.ds(pl.multiple_of(at * SMALL_ROWS, 8), SMALL_ROWS)], small_sem.at[at])
    columns = jnp.transpose(small[...])
    wide_lane = lax.broadcasted_iota(jnp.int32, (chunk, LANES), 1)

    def spread_gains(s):
        for unit in range(nz):
            at = s * SMALL_ROWS + unit
            part = jnp.broadcast_to(columns[0:chunk, at:at + 1], (chunk, LANES))
            gainb[s, unit * chunk:(unit + 1) * chunk] = part
            a, b, c = (p.astype(F32) for p in split3(part))
            tail = jnp.where(wide_lane == PARTS_AT + 1, a, 0.0)
            tail = jnp.where(wide_lane == PARTS_AT + 2, b, tail)
            tail = jnp.where(wide_lane == PARTS_AT + 3, c, tail)
            gtail[s, unit * chunk:(unit + 1) * chunk] = tail
        for half in range(HALVES):
            at = s * SMALL_ROWS + 16 + half
            part = jnp.broadcast_to(columns[0:chunk, at:at + 1], (chunk, LANES))
            gateb[s, half * chunk:(half + 1) * chunk] = part

    for s in range(sections):
        spread_gains(s)
        if s < 2:
            gather_until(2 + s)

    factor = jnp.where(lane < LIVE_PER_CLIP, factor, 0.0)

    def key_after(s):
        return len(GATHER_RELAYS[0]) + 2 * s + 1

    coeff = math.sqrt(2.0 / math.pi)
    state = None
    for s in range(sections):
        gather_all_of(s)
        weight = wbuf[s].reshape(deep, width)
        wt[...] = jnp.transpose(weight)
        for d in range(1, nt):
            at = lax.rem(t + d, nt)
            got(abuf.at[s, at], a_sem.at[s, at])
        values = abuf[s].reshape(deep, LANES).astype(F32)
        slice_mean = jnp.sum(values, axis=0, keepdims=True) * (1.0 / deep)
        centred = values - slice_mean
        slice_square = jnp.sum(centred * centred, axis=0, keepdims=True)
        operand = (centred * gainb[s] + gtail[s]).astype(BF16)
        partial = jnp.dot(wt[...], operand, preferred_element_type=F32)
        rounding = partial - partial.astype(BF16).astype(F32)
        all_lane = lax.broadcasted_iota(jnp.int32, (width, LANES), 1)
        partial = jnp.where(
            all_lane == PARTS_AT, pltpu.roll(rounding, LANES - 1, 1), partial
        ).astype(BF16)
        stats = stat_rows(slice_mean, slice_square)
        for to in range(nx):
            for half in range(HALVES):
                at = half * (width // HALVES) + to * chunk
                bsend[s, to, half * chunk:(half + 1) * chunk] = partial[at:at + chunk]
            bsend[s, to, own:own + TAIL] = stats
        for d in far_x:
            to = lax.rem(x + d, nx)
            put(bsend.at[s, to], bbuf.at[s, x], b_sem.at[s, x], "section", to)
        bbuf[s, x] = bsend[s, x]
        gather_until(key_after(s))
        for d in range(1, nx):
            at = lax.rem(x + d, nx)
            got(bbuf.at[s, at], b_sem.at[s, at])
        summed = jnp.zeros((own, LANES), F32)
        means, squares, sums = [], [], []
        for at in range(nx):
            block = bbuf[s, at, 0:own].astype(F32)
            summed += block
            sums.append(
                jnp.sum(jnp.where(lane >= PARTS_AT, block, 0.0), axis=1, keepdims=True)
            )
            one, two = joined(bbuf[s, at, own:own + TAIL])
            means.append(one)
            squares.append(two)
        mean = sum(means[1:], means[0]) * (1.0 / nx)
        square = sum(squares[1:], squares[0])
        for at in range(nx):
            square += deep * (means[at] - mean) * (means[at] - mean)
        inverse = lax.rsqrt(square * (1.0 / model) + EPS)
        total = jnp.where(lane < PARTS_AT, summed, 0.0)
        for at in range(nx):
            total += (means[at] - mean) * sums[at]
        v = total * inverse
        tanh = jnp.tanh(coeff * (v + 0.044715 * v * v * v))
        gelu = 0.5 * v * (1.0 + tanh)
        gate = gateb[s]
        state = (abuf[s, t].astype(F32) + gate * gelu).astype(BF16)
        if s < sections - 1:
            abuf[s + 1, t] = state
            a_sends(s + 1)
        slope = 0.5 * (1.0 + tanh) + 0.5 * v * (1.0 - tanh * tanh) * coeff * (
            1.0 + 3.0 * 0.044715 * v * v
        )
        projb[s] = v
        gelub[s] = gelu
        slopeb[s] = gate * slope
        meanb[s] = mean
        invb[s] = inverse
        ub[s] = jnp.broadcast_to(sum(sums[1:], sums[0]), (own, LANES))


    target = own_part(1).astype(F32)
    upstream = (factor * (state.astype(F32) - target)).astype(BF16).astype(F32)
    vacc[...] = jnp.zeros_like(vacc)

    def scatter_event(s, turn):
        reach = SCATTER_REACH[s]
        count = stages(reach)
        relay = count - turn
        mine = dwbuf[s, z].astype(F32) if relay == 0 else None
        ways = [
            (way, total, slots, sem)
            for way, total, (slots, sem) in lanes_of(s, (rs_up, rsu_sem), (rs_down, rsd_sem))
        ]
        for way, total, slots, sem in ways if turn > 0 else ():
            gone = relay * reach
            if gone >= total:
                continue
            children = range(gone + 1, min(gone + reach, total) + 1)
            for q in children:
                got(slots.at[s, q - 1], sem.at[s, q - 1])
            if relay > 0:
                mine = dwbuf[s, lax.rem(z + way * gone + nz, nz)].astype(F32)
            for q in children:
                mine = mine + slots[s, q - 1].astype(F32)
            if relay > 0:
                slots[s, gone] = mine.astype(BF16)
                to = lax.rem(z + way * reach + nz, nz)
                put(slots.at[s, gone], slots.at[s, gone - 1], sem.at[s, gone - 1], "dp", to)
        groups = (count, count - 1) if turn == 0 else (relay - 1,)
        for level in groups:
            for way, total, slots, sem in ways:
                for q in range(min(level * reach, total), (level - 1) * reach, -1):
                    if level >= 1 and (q % reach or q == total):
                        to = lax.rem(z + way * (q - (level - 1) * reach) + nz, nz)
                        term = dwbuf.at[s, lax.rem(z + way * q + nz, nz)]
                        put(term, slots.at[s, q - 1], sem.at[s, q - 1], "dp", to)
        if relay == 0:
            gw_send[s] = mine.astype(BF16)

            @pl.when(x != s)
            def _():
                put_to(gw_send.at[s], gw_in.at[x], gw_sem.at[x], s)

            @pl.when(x == s)
            def _():
                gw_in[x] = gw_send[s]

    def put_to(src, dst, recv, s):
        pltpu.make_async_remote_copy(
            src_ref=src, dst_ref=dst, send_sem=local_sem.at[1 + s], recv_sem=recv,
            device_id={"section": s}, device_id_type=MESH,
        ).start()

    back = sorted(
        (turn + SCATTER_START[s], s, turn)
        for s in range(sections) for turn in range(stages(SCATTER_REACH[s]) + 1)
    )

    def scatter_until(key):
        while back and back[0][0] <= key:
            _, s, turn = back.pop(0)
            scatter_event(s, turn)

    def add_gain(s, dnormed, xhat):
        vacc[0:own] = jnp.where(
            lane == 2 * s + 1, jnp.sum(dnormed * xhat, axis=1, keepdims=True), vacc[0:own]
        )

    for turn, s in enumerate(reversed(range(sections))):
        older = len(sends)
        dproj = (upstream * slopeb[s]).astype(BF16)
        exact = dproj.astype(F32)
        first_part = jnp.sum(exact * ub[s], axis=0, keepdims=True)
        second_part = jnp.sum(exact * projb[s], axis=0, keepdims=True)
        dbuf[s, x, 0:own] = dproj
        dbuf[s, x, own:own + TAIL] = stat_rows(first_part, second_part)
        for d in far_x:
            put(dbuf.at[s, x], dbuf.at[s, x], d_sem.at[s, x], "section", lax.rem(x + d, nx))
        if turn > 0:
            scatter_until(2 * turn - 1)
        vacc[0:own] = jnp.where(
            lane == 2 * s, jnp.sum(upstream * gelub[s], axis=1, keepdims=True), vacc[0:own]
        )
        if turn > 0:
            add_gain(s + 1, dnormed, xhat)
        mean, inverse = meanb[s], invb[s]
        normed = (
            (abuf[s].reshape(deep, LANES).astype(F32) - mean) * inverse * gainb[s]
        ).astype(BF16)
        for d in range(1, nx):
            at = lax.rem(x + d, nx)
            got(dbuf.at[s, at], d_sem.at[s, at])
        whole = jnp.concatenate(
            [dbuf[s, at, half * chunk:(half + 1) * chunk] for half in range(HALVES) for at in range(nx)],
            axis=0,
        )
        first_sum = jnp.zeros((1, LANES), F32)
        second_sum = jnp.zeros((1, LANES), F32)
        for at in range(nx):
            one, two = joined(dbuf[s, at, own:own + TAIL])
            first_sum += one
            second_sum += two
        def weight_term():
            term = lax.dot_general(
                normed, whole, (((1,), (1,)), ((), ())), preferred_element_type=F32
            )
            dwbuf[s] = term.astype(BF16).reshape(nz, chunk, width)

        if s == 0:
            weight_term()
            assert back.pop(0)[1:] == (0, 0)
            scatter_event(0, 0)
        product = jnp.dot(wbuf[s].reshape(deep, width), whole, preferred_element_type=F32).astype(BF16)
        stats = stat_rows(first_sum, second_sum)
        for to in range(nt):
            qsend[s, to, 0:own] = product[to * own:(to + 1) * own]
            qsend[s, to, own:own + TAIL] = stats
        for d in far_t:
            to = lax.rem(t + d, nt)
            put(qsend.at[s, to], qbuf.at[s, t], q_sem.at[s, t], "tensor", to)
        qbuf[s, t] = qsend[s, t]
        if s > 0:
            weight_term()
        scatter_until(2 * turn)
        finish_sends(older)
        for d in range(1, nt):
            at = lax.rem(t + d, nt)
            got(qbuf.at[s, at], q_sem.at[s, at])
        dnormed = jnp.zeros((own, LANES), F32)
        first_moment = jnp.zeros((1, LANES), F32)
        second_moment = jnp.zeros((1, LANES), F32)
        for at in range(nt):
            dnormed += qbuf[s, at, 0:own].astype(F32)
            one, two = joined(qbuf[s, at, own:own + TAIL])
            first_moment += one
            second_moment += two
        xhat = (abuf[s, t].astype(F32) - mean) * inverse
        if s > 0:
            gain = gainb[s, pl.ds(pl.multiple_of(t * own, 8), own)]
            change = dnormed * gain - first_moment * (1.0 / model) - xhat * (
                second_moment * (1.0 / model)
            )
            upstream = (upstream + inverse * change).astype(BF16).astype(F32)

    add_gain(0, dnormed, xhat)
    v1[member] = jnp.transpose(vacc[...])[0:8]
    for d in range(1, zb):
        to = group * zb + lax.rem(member + d, zb)
        put(v1.at[member], v1.at[member], v1_sem.at[member], "dp", to)
    scatter_until(SCATTER_START[0] + 1)
    finish_sends(len(sends) - 20)
    for d in range(1, zb):
        at = lax.rem(member + d, zb)
        got(v1.at[at], v1_sem.at[at])
    v2[group] = v1[0] + v1[1] + v1[2] + v1[3]
    for d in range(1, za):
        to = lax.rem(group + d, za) * zb + member
        put(v2.at[group], v2.at[group], v2_sem.at[group], "dp", to)
    scatter_until(SCATTER_START[0] + stages(SCATTER_REACH[0]) - 1)
    for d in range(1, za):
        at = lax.rem(group + d, za)
        got(v2.at[at], v2_sem.at[at])
    full = v2[0]
    for at in range(1, za):
        full = full + v2[at]
    v3[x] = full
    finish_sends(len(sends) - 6)
    for d in far_x:
        put(v3.at[x], v3.at[x], v3_sem.at[x], "section", lax.rem(x + d, nx))
    while back:
        _, s, turn = back.pop(0)
        scatter_event(s, turn)
    for d in range(1, nx):
        at = lax.rem(x + d, nx)
        got(v3.at[at], v3_sem.at[at])
    for at in range(nx):
        tile = v3[at]
        gate_row, gain_row = tile[0:1], tile[1:2]
        for s in range(1, sections):
            gate_row = jnp.where(x == s, tile[2 * s:2 * s + 1], gate_row)
            gain_row = jnp.where(x == s, tile[2 * s + 1:2 * s + 2], gain_row)
        for half in range(HALVES):
            to = half * (width // HALVES) + at * chunk
            row_part[0:1, to:to + chunk] = gate_row[:, half * chunk:(half + 1) * chunk]
            row_part[1:2, to:to + chunk] = gain_row[:, half * chunk:(half + 1) * chunk]
    for d in range(1, nx):
        at = lax.rem(x + d, nx)
        got(gw_in.at[at], gw_sem.at[at])
    gw_part[...] = gw_in[...]

    finish_sends(len(sends))
    for s in range(sections):
        @pl.when(x != s)
        def _():
            pltpu.make_async_remote_copy(
                src_ref=gw_send.at[s], dst_ref=gw_in.at[x], send_sem=local_sem.at[1 + s],
                recv_sem=gw_sem.at[x], device_id={"section": s}, device_id_type=MESH,
            ).wait_send()


def results(parts, rows, weight_out, gain_out, gate_out):
    chunk = parts.shape[1]
    for at in range(parts.shape[0]):
        weight_out[0, at * chunk:(at + 1) * chunk] = parts[at].astype(F32)
    gate_out[...] = rows[0:1]
    gain_out[...] = rows[1:2]


def local(inputs, velocity, weights, gains, gates, lengths, steps):
    nx, nt, nz = lax.axis_size("section"), lax.axis_size("tensor"), lax.axis_size("dp")
    sections = nx
    width = inputs.shape[2]
    chunk = width // (HALVES * nx)
    own = HALVES * chunk
    deep = nt * own
    ups, downs = nz // 2, nz // 2 - 1
    block = own + TAIL
    sends = (
        2 * (nx - 1) + 2 * sections * (ups + downs) + 2 * sections * (nt - 1)
        + 2 * sections * (nx - 1) + 3 + nz // 4 - 1 + nx - 1
    )
    dma = pltpu.SemaphoreType.DMA
    vmem = pl.BlockSpec(memory_space=pltpu.VMEM)
    anywhere = pl.BlockSpec(memory_space=pltpu.HBM)
    parts, rows = pl.pallas_call(
        functools.partial(kernel, nx, nt, nz),
        out_shape=(
            jax.ShapeDtypeStruct((nx, chunk, width), BF16),
            jax.ShapeDtypeStruct((2, width), F32),
        ),
        in_specs=[anywhere] * 7,
        out_specs=(vmem, vmem),
        scratch_shapes=[
            pltpu.VMEM(inputs.shape, BF16),
            pltpu.VMEM(velocity.shape, BF16),
            pltpu.VMEM(gains.shape, F32),
            pltpu.VMEM(gates.shape, F32),
            pltpu.VMEM(lengths.shape, jnp.int32),
            pltpu.VMEM(steps.shape, jnp.int32),
            pltpu.VMEM((sections, nz, chunk, width), BF16),
            pltpu.VMEM((width, deep), BF16),
            pltpu.VMEM((nx, SMALL_ROWS, LANES), F32),
            pltpu.VMEM((LANES, LANES), F32),
            pltpu.VMEM((sections, deep, LANES), F32),
            pltpu.VMEM((sections, deep, LANES), F32),
            pltpu.VMEM((sections, own, LANES), F32),
            pltpu.VMEM((2, HALVES * nx, chunk, LANES), BF16),
            pltpu.VMEM((sections, nt, own, LANES), BF16),
            pltpu.VMEM((sections, nx, block, LANES), BF16),
            pltpu.VMEM((sections, nx, block, LANES), BF16),
            pltpu.VMEM((sections, own, LANES), F32),
            pltpu.VMEM((sections, own, LANES), F32),
            pltpu.VMEM((sections, own, LANES), F32),
            pltpu.VMEM((sections, 1, LANES), F32),
            pltpu.VMEM((sections, 1, LANES), F32),
            pltpu.VMEM((sections, own, LANES), F32),
            pltpu.VMEM((sections, nx, block, LANES), BF16),
            pltpu.VMEM((sections, nt, block, LANES), BF16),
            pltpu.VMEM((sections, nt, block, LANES), BF16),
            pltpu.VMEM((sections, nz, chunk, width), BF16),
            pltpu.VMEM((sections, ups, chunk, width), BF16),
            pltpu.VMEM((sections, ups, chunk, width), BF16),
            pltpu.VMEM((sections, chunk, width), BF16),
            pltpu.VMEM((nx, chunk, width), BF16),
            pltpu.VMEM((LANES, LANES), F32),
            pltpu.VMEM((4, 8, LANES), F32),
            pltpu.VMEM((max(nz // 4, 1), 8, LANES), F32),
            pltpu.VMEM((nx, 8, LANES), F32),
            dma((sends,)),
            dma((1 + sections,)),
            dma((6,)),
            dma((nx,)),
            dma((nx,)),
            dma((sections, ups)),
            dma((sections, ups)),
            dma((sections, nt)),
            dma((sections, nx)),
            dma((sections, nx)),
            dma((sections, nt)),
            dma((sections, ups)),
            dma((sections, ups)),
            dma((nx,)),
            dma((4,)),
            dma((max(nz // 4, 1),)),
            dma((nx,)),
        ],
        compiler_params=pltpu.CompilerParams(
            collective_id=0, has_side_effects=True, vmem_limit_bytes=64 * 1024 * 1024
        ),
        name="sections",
    )(weights, inputs, velocity, gains, gates, lengths, steps)
    return pl.pallas_call(
        results,
        out_shape=(
            jax.ShapeDtypeStruct((1, nx * chunk, width), F32),
            jax.ShapeDtypeStruct((1, width), F32),
            jax.ShapeDtypeStruct((1, width), F32),
        ),
        in_specs=[vmem, vmem],
        out_specs=(vmem, vmem, vmem),
        name="results",
    )(parts, rows)


def solution(mesh):
    placed = (
        P(None, "dp", "tensor"),
        P(None, "dp", "tensor"),
        P("section", "dp", "tensor"),
        P("section", None),
        P("section", "tensor"),
        P("dp", None),
        P("dp", None),
    )

    def whole(*args):
        return jax.shard_map(
            local, mesh=mesh, in_specs=placed,
            out_specs=(P("section", "dp", "tensor"), P("section", "tensor"), P("section", "tensor")),
            check_vma=False,
        )(*args)

    return whole
```
